32 devices in a mesh: groups: 2 (over y), tok: 4 (over x, core), voc: 4 (over z).
Axes of the slice: x: 2, y: 2, z: 4, core: 2. Of those that a mesh axis runs over, the one named last changes fastest.
Arguments:
- hidden: bfloat16 [4096, 2048], P(('groups', 'tok', 'voc')), parts along dimension 0, may hold values from -210 to 210
- head: bfloat16 [163840, 2048], P(('tok', 'voc')), may hold values from -0.125 to 0.125
- block_ids: int32 [4096, 8], P(('groups', 'tok', 'voc')), parts along dimension 0, may hold values from 0 to 1279, all different within a row; in each aligned block of 128 rows (0 to 127, 128 to 255, ...) at most 2 rows name the same one
- live_counts: int32 [4096], P(('groups', 'tok', 'voc')), parts along dimension 0, may hold values from 1 to 8, as said below
- teacher: bfloat16 [4096, 8, 128], P(('groups', 'tok', 'voc')), parts along dimension 0, may hold values from -15 to 215
Outputs:
- hidden_grad: bfloat16 [4096, 2048], P(('groups', 'tok', 'voc')), parts along dimension 0
- head_grad: bfloat16 [327680, 2048], P(('groups', 'tok', 'voc')), parts along dimension 0
- token_loss: float32 [4096], P(('groups', 'tok', 'voc')), parts along dimension 0
The draws below stay inside these ranges and needn't reach their ends.
There are 2 independent parts, one for each index of `groups`. The reference program is written for one: setup_inputs(seed, part) draws one part's arguments, and reference() takes and returns one part's arrays. A program takes and returns all parts, laid end to end along the dimension named above; an argument that names none is the same for every part. Nothing has to cross between parts.
Inputs may be any that keep to these rules, and one draw needn't show every extreme that they name: `block_ids`: each token lists 8 different blocks. Among the list entries of one device's 128 tokens (aligned runs), no block is named more than 2 times, live or not, and some block is named exactly 2 times on some devices. Entries 0 to live_counts - 1 of a token's list are live; the others carry no weight. Some device has all of its tokens' entries live.
All inputs are finite; a program needn't handle non-finite values.
Results may differ from the reference program's by a relative error of at most 0.0059.
Values may be sent and summed in bfloat16 or wider, within the bound.
No kernel may reach another device: no remote copies, remote signals or barrier semaphores. Data moves between devices by JAX's collectives and lax.ppermute only.
A program may use at most 256 MiB of HBM per device.

```python
import math
import jax
import jax.numpy as jnp
import numpy as np
from jax import lax

D = 2048
V = 163840
BLOCK = 128
K = 8
TOK_DEV = 128
NB = 1280
C = 2
TOKENS = 2048


def draw_hidden(key, part):
    key = jax.random.fold_in(key, 11)
    values = jnp.clip(jax.random.normal(key, (TOKENS, D), jnp.float32), -6.0, 6.0)
    return values.astype(jnp.bfloat16)


def draw_live_counts(key, part):
    key = jax.random.fold_in(key, 23)
    position = jnp.arange(TOKENS, dtype=jnp.int32)
    device_index = position // TOK_DEV
    device_total = TOKENS // TOK_DEV
    lower = jnp.maximum(1, K - (K - 1) * device_index // max(device_total - 1, 1))
    span = jnp.where(device_index == 0, 1, max(K // 2, 1))
    raw_bits = jax.random.randint(key, (TOKENS,), 0, 1 << 20, dtype=jnp.int32)
    counts = jnp.minimum(K, lower + raw_bits % span)
    counts = jnp.where(position == TOKENS - 1, 1, counts)
    return counts.astype(jnp.int32)


def draw_teacher(key, part):
    key = jax.random.fold_in(key, 37)
    keys = jax.random.split(key, 1)
    shape = (TOKENS, K, BLOCK)
    values = jnp.clip(3.0 * jax.random.normal(keys[0], shape, jnp.float32), -15.0, 15.0)
    return values.astype(jnp.bfloat16)


def block_levels(own_key, shape, pieces, least, top_value):
    level, own = 1.0, jax.random.fold_in(own_key, 6)
    for dim, shards_of in pieces:
        draws = jnp.exp(jax.random.uniform(jax.random.fold_in(own, dim), (shards_of,), jnp.float32, least / len(pieces), top_value / len(pieces)))
        level = level * jnp.repeat(draws, shape[dim] // shards_of).reshape([-1 if axis == dim else 1 for axis in range(len(shape))])
    return level


def shared_out(stream_key, own, number, rows, number_of, top, bound, skew):
    ranking = jax.random.permutation(stream_key, number_of)
    heavy_load, usual = portions_of(number_of, rows * top, bound, skew, True), portions_of(number_of, rows * top, bound, skew, False)
    places = jnp.arange(number_of)

    def named(sizes, offset_by):
        used = int((sizes > 0).sum())
        fixed = max(1, used // 4)
        shifted = fixed + (places - fixed + offset_by * (used - fixed)) % max(1, number_of - fixed)
        return jnp.zeros((number_of,), jnp.int32).at[ranking[jnp.where(places < fixed, places, shifted)]].set(jnp.asarray(sizes, jnp.int32))

    sizes = jnp.where(number % 4 == 0, named(heavy_load, number // 4), named(usual, number - number // 4 - 1))
    mixed = jax.random.permutation(jax.random.fold_in(own, 3), number_of)
    donor, sink = mixed[0:number_of // 2 * 2:2], mixed[1:number_of // 2 * 2:2]
    margin = jnp.minimum(sizes[donor] - 1, bound - sizes[sink]) // 2
    margin = jnp.where((donor == ranking[0]) | (sink == ranking[0]) | (sizes[sink] == 0), 0, jnp.maximum(margin, 0))
    shifted = jax.random.randint(jax.random.fold_in(own, 4), (number_of // 2,), 0, 1 << 20) % (margin + 1)
    sizes = sizes.at[donor].add(-shifted).at[sink].add(shifted)
    items = jnp.searchsorted(jnp.cumsum(sizes), jnp.arange(rows * top), side="right").astype(jnp.int32)
    table = items.reshape(top, rows).T
    table = table[jax.random.permutation(jax.random.fold_in(own, 1), rows)]
    offset_by = jax.random.randint(jax.random.fold_in(own, 2), (rows, 1), 0, top)
    return jnp.take_along_axis(table, (jnp.arange(top)[None, :] + offset_by) % top, axis=1)


def portions_of(count, total, limit, skew, full):
    weights = [(1 << 20) // math.isqrt(standing ** skew) + 1 for standing in range(1, count + 1)]
    largest = limit if full else min(limit, max(-(-total // count), total * weights[0] // sum(weights)))
    least = 1 if total - largest >= count - 1 else 0
    holding, surplus = [largest] + [least] * (count - 1), total - largest - least * (count - 1)
    while surplus > 0:
        movable = [i for i in range(1, count) if holding[i] < largest] or [i for i in range(1, count) if holding[i] < limit]
        mass, remaining = sum([weights[i] for i in movable]), surplus
        for i in movable:
            addition = min(limit - holding[i], max(1, remaining * weights[i] // mass), surplus)
            holding[i] = holding[i] + addition
            surplus = surplus - addition
    return np.array(holding)


def bell_draw(own_key, extent, scale, bound, pieces=(), kind=jnp.bfloat16):
    entries = scale * jax.random.normal(own_key, extent, jnp.float32)
    if pieces:
        entries = entries * block_levels(own_key, extent, pieces, -0.22, 0.18)
    return jnp.clip(entries, -bound, bound).astype(kind)


def setup_inputs(seed: int = 0, part: int = 0) -> dict:
    arg_keys = jax.random.split(jax.random.key(seed), 6)
    part_keys = jax.random.split(jax.random.fold_in(arg_keys[5], part), 6)
    hidden = draw_hidden(jax.random.fold_in(jax.random.fold_in(arg_keys[5], part), 71), part)
    head = bell_draw(arg_keys[1], (V, D), D ** -0.5, 0.125, ((0, 16),))
    block_ids_keys = jax.random.split(jax.random.fold_in(part_keys[2], 1), TOKENS // TOK_DEV)
    block_ids_turns = jax.random.permutation(jax.random.fold_in(part_keys[2], 3), TOKENS // TOK_DEV)
    block_ids = jax.vmap(lambda own, number: shared_out(jax.random.fold_in(part_keys[2], 2), own, number, TOK_DEV, NB, K, C, 2))(block_ids_keys, block_ids_turns).reshape((TOKENS, K))
    live_counts = draw_live_counts(jax.random.fold_in(jax.random.fold_in(arg_keys[5], part), 71), part)
    teacher = draw_teacher(jax.random.fold_in(jax.random.fold_in(arg_keys[5], part), 71), part)
    return dict(hidden=hidden, head=head, block_ids=block_ids, live_counts=live_counts, teacher=teacher)


blocks_per_turn = 16


def log_softmax_rows(values):
    top = jnp.max(values, axis=-1, keepdims=True)
    return values - top - jnp.log(jnp.sum(jnp.exp(values - top), axis=-1, keepdims=True))


def reference(hidden, head, block_ids, live_counts, teacher):
    slot_total = TOKENS * K
    scale = jnp.float32(TOKENS) / jnp.sum(live_counts).astype(jnp.float32)
    flat_ids = block_ids.reshape(slot_total).astype(jnp.int32)
    live = (jnp.arange(K, dtype=jnp.int32)[None, :] < live_counts[:, None]).reshape(slot_total)
    weights_all = jnp.where(live, scale, jnp.float32(0.0))
    order = jnp.argsort(flat_ids, stable=True).astype(jnp.int32)
    sorted_ids = flat_ids[order]
    per_block = jnp.zeros((NB,), jnp.int32).at[flat_ids].add(1)
    starts = jnp.cumsum(per_block).astype(jnp.int32) - per_block
    ranks = jnp.arange(slot_total, dtype=jnp.int32) - starts[sorted_ids]
    capacity = C * (TOKENS // TOK_DEV)
    table = jnp.full((NB, capacity), slot_total, jnp.int32).at[sorted_ids, ranks].set(order)
    hidden_pad = jnp.concatenate([hidden, jnp.zeros((1, D), hidden.dtype)], axis=0)
    teacher_pad = jnp.concatenate([teacher.reshape(slot_total, BLOCK), jnp.zeros((1, BLOCK), teacher.dtype)], axis=0)
    weight_pad = jnp.concatenate([weights_all, jnp.zeros((1,), jnp.float32)], axis=0)
    head_blocks = head.reshape(NB, BLOCK, D)

    def one_turn(carry, turn):
        grad_rows, loss_rows = carry
        start = (turn * blocks_per_turn).astype(jnp.int32)
        slot_table = lax.dynamic_slice_in_dim(table, start, blocks_per_turn, 0)
        token_rows = slot_table // K
        gathered = hidden_pad[token_rows].astype(jnp.float32)
        block_weights = lax.dynamic_slice_in_dim(head_blocks, start, blocks_per_turn, 0).astype(jnp.float32)
        logits = jnp.einsum("gcd,gvd->gcv", gathered, block_weights)
        student_log = log_softmax_rows(logits)
        teacher_log = log_softmax_rows(teacher_pad[slot_table].astype(jnp.float32))
        teacher_prob = jnp.exp(teacher_log)
        weight = weight_pad[slot_table]
        divergence = (weight * jnp.sum(teacher_prob * (teacher_log - student_log), axis=-1)).astype(jnp.bfloat16)
        divergence = lax.optimization_barrier(divergence).astype(jnp.float32)
        grad_logits = (BLOCK * weight[..., None] * (jnp.exp(student_log) - teacher_prob)).astype(jnp.bfloat16)
        grad_wide = lax.optimization_barrier(grad_logits).astype(jnp.float32)
        block_grad = jnp.einsum("gcv,gcd->gvd", grad_wide, gathered).astype(jnp.bfloat16)
        slot_grad = jnp.einsum("gcv,gvd->gcd", grad_wide, block_weights).astype(jnp.bfloat16)
        slot_grad = lax.optimization_barrier(slot_grad).astype(jnp.float32)
        flat_rows = token_rows.reshape(-1)
        grad_rows = grad_rows.at[flat_rows].add(slot_grad.reshape(-1, D))
        loss_rows = loss_rows.at[flat_rows].add(divergence.reshape(-1))
        return (grad_rows, loss_rows), block_grad

    init = (jnp.zeros((TOKENS + 1, D), jnp.float32), jnp.zeros((TOKENS + 1,), jnp.float32))
    turns = jnp.arange(NB // blocks_per_turn, dtype=jnp.int32)
    (grad_rows, loss_rows), block_grads = lax.scan(one_turn, init, turns)
    return grad_rows[:TOKENS].astype(jnp.bfloat16), block_grads.reshape(V, D), loss_rows[:TOKENS]
```

```python
import jax
import jax.numpy as jnp
from jax import lax
from jax.sharding import PartitionSpec as P

BLOCK = 128
C = 2
AXES = ("tok", "voc")


def log_softmax_rows(values):
    top = jnp.max(values, axis=-1, keepdims=True)
    return values - top - jnp.log(jnp.sum(jnp.exp(values - top), axis=-1, keepdims=True))


def on_device(hidden, head, block_ids, live_counts, teacher):
    devices = lax.axis_size(AXES)
    tokens, list_width = block_ids.shape
    width = hidden.shape[1]
    local_blocks = head.shape[0] // BLOCK
    entries = tokens * list_width
    bucket = local_blocks * C
    flat_ids = block_ids.reshape(entries)
    position = jnp.arange(entries, dtype=jnp.int32)
    earlier = (flat_ids[:, None] == flat_ids[None, :]) & (position[:, None] > position[None, :])
    ranks = jnp.sum(earlier, axis=1, dtype=jnp.int32)
    live = (jnp.arange(list_width, dtype=jnp.int32)[None, :] < live_counts[:, None]).reshape(entries)
    rows = jnp.where(live, flat_ids * C + ranks, -1)

    all_hidden = lax.all_gather(hidden, AXES, axis=0)
    all_rows = lax.all_gather(rows, AXES, axis=0)
    slots = jnp.arange(devices * bucket, dtype=jnp.int32)
    place = (slots[:, None] == rows[None, :]).astype(jnp.bfloat16)
    send_teacher = jnp.dot(
        place, teacher.reshape(entries, BLOCK), preferred_element_type=jnp.float32
    ).astype(jnp.bfloat16)
    got_teacher = lax.all_to_all(
        send_teacher.reshape(devices, bucket, BLOCK), AXES, split_axis=0, concat_axis=0, tiled=True
    )

    me = lax.axis_index(AXES)
    live_total = jnp.sum(all_rows >= 0, dtype=jnp.int32)
    scale = jnp.float32(tokens * devices) / live_total.astype(jnp.float32)
    own = (all_rows - me * bucket).reshape(devices, 1, tokens, list_width)
    here = jnp.arange(bucket, dtype=jnp.int32)[None, :, None, None]
    pick = jnp.any(own == here, axis=-1)
    weight = jnp.where(jnp.any(pick, axis=-1), scale, jnp.float32(0.0))
    pick = pick.astype(jnp.bfloat16)

    got_hidden = jnp.einsum("sgt,std->sgd", pick, all_hidden, preferred_element_type=jnp.float32)
    got_hidden = got_hidden.astype(jnp.bfloat16).reshape(devices, local_blocks, C, width)
    blocks = head.reshape(local_blocks, BLOCK, width)
    logits = jnp.einsum("sbcd,bvd->sbcv", got_hidden, blocks, preferred_element_type=jnp.float32)
    student_log = log_softmax_rows(logits)
    teacher_log = log_softmax_rows(
        got_teacher.reshape(devices, local_blocks, C, BLOCK).astype(jnp.float32)
    )
    teacher_prob = jnp.exp(teacher_log)
    weight = weight.reshape(devices, local_blocks, C)
    divergence = (weight * jnp.sum(teacher_prob * (teacher_log - student_log), axis=-1)).astype(
        jnp.bfloat16
    )
    grad_logits = (BLOCK * weight[..., None] * (jnp.exp(student_log) - teacher_prob)).astype(
        jnp.bfloat16
    )
    slot_grad = jnp.einsum(
        "sbcv,bvd->sbcd", grad_logits, blocks, preferred_element_type=jnp.float32
    ).astype(jnp.bfloat16)
    part = jnp.einsum(
        "sgt,sgd->std",
        pick,
        slot_grad.reshape(devices, bucket, width),
        preferred_element_type=jnp.float32,
    ).astype(jnp.bfloat16)
    hidden_grad = lax.psum_scatter(
        part.reshape(devices * tokens, width), AXES, scatter_dimension=0, tiled=True
    )
    summed = jnp.einsum(
        "sbcv,sbcd->bvd", grad_logits, got_hidden, preferred_element_type=jnp.float32
    )
    head_grad = summed.astype(jnp.bfloat16).reshape(local_blocks * BLOCK, width)
    loss_part = jnp.sum(
        pick.astype(jnp.float32) * divergence.astype(jnp.float32).reshape(devices, bucket, 1), axis=1
    )
    token_loss = lax.psum_scatter(
        loss_part.reshape(devices * tokens), AXES, scatter_dimension=0, tiled=True
    )
    return hidden_grad, head_grad, token_loss


def solution(mesh):
    tokens_on = ("groups", "tok", "voc")
    return jax.shard_map(
        on_device,
        mesh=mesh,
        in_specs=(
            P(tokens_on, None),
            P(AXES, None),
            P(tokens_on, None),
            P(tokens_on),
            P(tokens_on, None, None),
        ),
        out_specs=(P(tokens_on, None), P(tokens_on, None), P(tokens_on)),
        check_vma=False,
    )
```

```python
import functools

import jax
import jax.numpy as jnp
import numpy as np
from jax import lax
from jax.experimental import pallas as pl
from jax.experimental.pallas import tpu as pltpu
from jax.sharding import Mesh
from jax.sharding import PartitionSpec as P

BLOCK = 128
LANES = 128
C = 2
QUAD = 4
ROWS = QUAD * C
COLS = 256
ALL = ("x", "core", "voc")
CHIPS = ("x", "voc")
RING_MOST = 8
VMEM_LIMIT = 52 * 1024 * 1024
NT = (((1,), (1,)), ((), ()))


def call(kernel, name, grid, ins, outs, shapes, flops, moved, scratch=(), aliases=None):
    return pl.pallas_call(
        kernel,
        grid=grid,
        in_specs=ins,
        out_specs=outs,
        out_shape=shapes,
        scratch_shapes=scratch,
        input_output_aliases=aliases or {},
        compiler_params=pltpu.CompilerParams(
            dimension_semantics=("arbitrary",) * len(grid), vmem_limit_bytes=VMEM_LIMIT
        ),
        cost_estimate=pl.CostEstimate(flops=flops, bytes_accessed=moved, transcendentals=0),
        name=name,
    )


def place_kernel(layout, pick_ref, *refs):
    *held, out_ref = refs
    width = out_ref.shape[1]
    blocks = out_ref.shape[0] // (2 * ROWS)
    for start in range(0, width, COLS):
        quads = []
        for quad in range(2):
            values = []
            for pieces in layout[quad * QUAD : (quad + 1) * QUAD]:
                at = start
                for number in pieces:
                    if at < held[number].shape[1]:
                        values.append(held[number][:, at : at + COLS])
                        break
                    at -= held[number].shape[1]
            rows = jnp.dot(
                pick_ref[quad], jnp.concatenate(values, axis=0), preferred_element_type=jnp.float32
            )
            quads.append(rows.reshape(blocks, ROWS, COLS))
        both = jnp.concatenate(quads, axis=1).reshape(blocks * 2 * ROWS, COLS)
        out_ref[:, start : start + COLS] = both.astype(jnp.bfloat16)


def in_block(shape, axis, pairs, joint):
    slot = lax.broadcasted_iota(jnp.int32, shape, axis)
    group = pairs * joint * 2 * ROWS
    return slot // group * joint + slot % (joint * 2 * ROWS) // (2 * ROWS)


def joint_rows(x_refs, first, joint, columns=slice(None)):
    rows = slice(first * 2 * ROWS, (first + joint) * 2 * ROWS)
    return [ref[rows, columns] for ref in x_refs]


def sum_quad(spread_ref, rows_ref, quad, columns):
    blocks = rows_ref.shape[0]
    rows = rows_ref[:, quad * ROWS : (quad + 1) * ROWS, columns]
    rows = rows.reshape(blocks * ROWS, rows.shape[-1]).astype(jnp.bfloat16)
    return jnp.dot(spread_ref[quad], rows, preferred_element_type=jnp.float32)


def main_kernel(turn, steps, pairs, sums, scale_ref, head_ref, teacher_ref, spread_ref, *refs):
    x_refs = refs[:pairs]
    grad_ref, *loss_ref = refs[pairs:-2]
    rows_ref, slot_loss_ref = refs[-2:]
    step = pl.program_id(0)
    origin = step * turn if sums else 0
    scale = scale_ref[0]
    joint = 2 if turn % 2 == 0 else 1
    group = pairs * joint * 2 * ROWS
    own_block = in_block((group, BLOCK), 0, pairs, joint)
    logits = []
    for first in range(0, turn, joint):
        product = lax.dot_general(
            jnp.concatenate(joint_rows(x_refs, first, joint), axis=0),
            head_ref[first * BLOCK : (first + joint) * BLOCK, :],
            NT,
            preferred_element_type=jnp.float32,
        )
        part = product[:, :BLOCK]
        for k in range(1, joint):
            part = jnp.where(own_block == k, product[:, k * BLOCK : (k + 1) * BLOCK], part)
        logits.append(part)
    logits = jnp.concatenate(logits, axis=0)

    def log_softmax(values):
        top = jnp.max(values, axis=-1, keepdims=True)
        return values - top - jnp.log(jnp.sum(jnp.exp(values - top), axis=-1, keepdims=True))

    student_log = log_softmax(logits)
    teacher_log = log_softmax(teacher_ref[...].astype(jnp.float32))
    teacher_prob = jnp.exp(teacher_log)
    loss = scale * jnp.sum(teacher_prob * (teacher_log - student_log), axis=-1, keepdims=True)
    loss = jnp.broadcast_to(loss, logits.shape)
    grad = BLOCK * scale * (jnp.exp(student_log) - teacher_prob)
    grad_ref[...] = grad.T.astype(jnp.bfloat16)
    grad = grad.astype(jnp.bfloat16)

    for first in range(0, turn, joint):
        here = slice(first * pairs * 2 * ROWS, (first + joint) * pairs * 2 * ROWS)
        lines = [
            jnp.where(own_block == k, grad[here], jnp.zeros_like(grad[here])) for k in range(joint)
        ]
        grads = jnp.dot(
            jnp.concatenate(lines, axis=1),
            head_ref[first * BLOCK : (first + joint) * BLOCK, :],
            preferred_element_type=jnp.float32,
        )
        for pair in range(pairs):
            to = slice(pair * 2 * ROWS, (pair + 1) * 2 * ROWS)
            for k in range(joint):
                start = (pair * joint + k) * 2 * ROWS
                rows_ref[origin + first + k, to, :] = grads[start : start + 2 * ROWS].astype(
                    rows_ref.dtype
                )
                start += here.start
                slot_loss_ref[origin + first + k, to, :] = loss[start : start + 2 * ROWS]

    if not sums:
        return
    loss_ref, *part_refs = loss_ref

    @pl.when(step == steps - 1)
    def _():
        half = spread_ref.shape[1] // 2
        for quad in range(2 * pairs):
            loss_ref[quad] = sum_quad(spread_ref, slot_loss_ref, quad, slice(0, BLOCK))
            for start in range(0, rows_ref.shape[-1], COLS):
                columns = slice(start, start + COLS)
                total = sum_quad(spread_ref, rows_ref, quad, columns).astype(jnp.bfloat16)
                part_refs[quad // 2][quad % 2, :, columns] = total[:half]
                part_refs[pairs + quad // 2][quad % 2, :, columns] = total[half:]


def head_kernel(turn, splits, pairs, grad_ref, *refs):
    x_refs, (out_ref, mark_ref) = refs[:pairs], refs[-2:]
    joint = 2 if turn % 2 == 0 else 1
    slots = grad_ref.shape[1]
    share = turn // splits
    place = in_block((1, slots), 1, pairs, joint) - pl.program_id(0) % splits * share
    grad = grad_ref[...]
    spaced = [grad * (place == index).astype(jnp.bfloat16) for index in range(share)]
    spaced = jnp.concatenate(spaced, axis=0)
    for start in range(0, out_ref.shape[1], COLS):
        columns = slice(start, start + COLS)
        rows = [
            piece
            for first in range(0, turn, joint)
            for piece in joint_rows(x_refs, first, joint, columns)
        ]
        out_ref[:, columns] = jnp.dot(
            spaced, jnp.concatenate(rows, axis=0), preferred_element_type=jnp.float32
        ).astype(jnp.bfloat16)
    mark_ref[...] = jnp.zeros_like(mark_ref)


def add_kernel(*refs):
    *terms, right_ref, left_ref = refs
    for way, out_ref in enumerate((right_ref, left_ref)):
        total = sum(ref[...].reshape(out_ref.shape).astype(jnp.float32) for ref in terms[way::2])
        out_ref[...] = total.astype(jnp.bfloat16)


def ring_order(rows, columns):
    order = []
    for r in range(rows):
        line = [r * columns + c for c in range(columns)]
        order += line if r % 2 == 0 else line[::-1]
    return order


def arrivals(chips):
    near = [0]
    for step in range(1, chips // 2):
        near += [-step, step]
    return near + [chips // 2]


def after(value, *others):
    return lax.optimization_barrier((value, *others))[0]


class Ring:
    def __init__(self, hidden, order):
        chips = len(order)
        self.chips = chips
        self.ways = [
            [(order[p], order[(p + way) % chips]) for p in range(chips)] for way in (1, -1)
        ]
        self.moving = [hidden, hidden]
        self.got = [self.both([hidden])]

    def both(self, pieces):
        return pieces, [lax.ppermute(piece, "core", [(0, 1), (1, 0)]) for piece in pieces]

    def step(self):
        self.moving = [lax.ppermute(m, CHIPS, way) for m, way in zip(self.moving, self.ways)]
        self.got += [self.both([m]) for m in self.moving]

    def last(self):
        half = self.moving[0].shape[1] // 2
        parts = [self.moving[0][:, :half], self.moving[1][:, half:]]
        self.moving = [lax.ppermute(p, CHIPS, way) for p, way in zip(parts, self.ways)]

    def finish(self, *behind):
        self.got += [self.both([after(m, *behind) for m in self.moving])]


def gather_whole(hidden):
    chips = lax.axis_size(CHIPS)
    own = lax.all_gather(hidden, CHIPS, axis=0)
    other = lax.ppermute(own, "core", [(0, 1), (1, 0)])
    return [([own[chip]], [other[chip]]) for chip in range(chips)]


def on_device(hidden, head, block_ids, live_counts, teacher):
    across, down = lax.axis_size("x"), lax.axis_size("voc")
    chips = across * down
    devices = 2 * chips
    pairs = chips // 4
    tokens, list_width = block_ids.shape
    width = hidden.shape[1]
    blocks = head.shape[0] // BLOCK
    even = [n for n in range(2, 9, 2) if blocks % n == 0]
    turn = max(even) if even else 1
    steps = blocks // turn
    entries = tokens * list_width
    bucket = blocks * C
    per_block = devices * C
    core = lax.axis_index("core")
    ring = chips <= RING_MOST
    order = ring_order(across, down)
    if ring:
        circle = Ring(hidden, order)
        for _ in range(chips // 2 - 1):
            circle.step()
        circle.last()
        held = circle.got
        offsets = np.array(arrivals(chips))
        places = np.argsort(np.array(order))
        spot = jnp.asarray(places, jnp.int32)[lax.axis_index(CHIPS)]
        chip_of = jnp.asarray(np.array(order), jnp.int32)[(spot + offsets) % chips]
    else:
        held = gather_whole(hidden)
        offsets = np.arange(chips)
        chip_of = jnp.arange(chips, dtype=jnp.int32)

    flat_ids = block_ids.reshape(entries)
    position = jnp.arange(entries, dtype=jnp.int32)
    earlier = (flat_ids[:, None] == flat_ids[None, :]) & (position[:, None] > position[None, :])
    ranks = jnp.sum(earlier, axis=1, dtype=jnp.int32)
    live = (jnp.arange(list_width, dtype=jnp.int32)[None, :] < live_counts[:, None]).reshape(entries)
    map_rows = -(-bucket // BLOCK)
    meta_at = -(-bucket // 16) * 16
    deep = meta_at + -(-(map_rows + 2) // 16) * 16
    rows = flat_ids // blocks * deep + ranks * blocks + flat_ids % blocks
    slots = jnp.arange(devices * deep, dtype=jnp.int32)
    place = (slots[:, None] == rows[None, :]).astype(jnp.bfloat16)
    send_teacher = jnp.dot(
        place, teacher.reshape(entries, BLOCK), preferred_element_type=jnp.float32
    ).astype(jnp.bfloat16)
    named = jnp.where(live, position // list_width + 1, 0)
    send_map = jnp.sum(jnp.where(rows[:, None] == slots[None, :], named[:, None], 0), axis=0)
    send_map = send_map.reshape(devices, deep)[:, :bucket]
    send_map = jnp.pad(send_map, ((0, 0), (0, map_rows * BLOCK - bucket)))
    live_sum = jnp.sum(live_counts)
    send_meta = jnp.concatenate(
        [
            send_map.reshape(devices, map_rows, BLOCK),
            jnp.broadcast_to(live_sum // 256, (devices, 1, BLOCK)),
            jnp.broadcast_to(live_sum % 256, (devices, 1, BLOCK)),
            jnp.zeros((devices, deep - meta_at - map_rows - 2, BLOCK), jnp.int32),
        ],
        axis=1,
    ).astype(jnp.bfloat16)
    sent = lax.dynamic_update_slice(
        send_teacher.reshape(devices, deep, BLOCK), send_meta, (0, meta_at, 0)
    )
    got = lax.all_to_all(sent, ALL, split_axis=0, concat_axis=0, tiled=True)

    lanes = jnp.stack([core, 1 - core])
    pair_of = chip_of.reshape(chips // 2, 1, 2)
    source_of = (pair_of // down * 2 + lanes[None, :, None]) * down + pair_of % down
    source_of = source_of.reshape(devices)
    got = jnp.take(got, source_of, axis=0)
    meta = got[:, meta_at:].astype(jnp.int32)
    live_total = jnp.sum(meta[:, map_rows, 0] * 256 + meta[:, map_rows + 1, 0])
    scale = jnp.float32(tokens * devices) / live_total.astype(jnp.float32)
    slot_map = meta[:, :map_rows].reshape(devices, map_rows * BLOCK)[:, :bucket]
    quads = devices // QUAD
    slot_map = slot_map.reshape(quads, QUAD, C, blocks)
    offset = jnp.arange(QUAD, dtype=jnp.int32)[None, :, None, None] * tokens - 1
    slot_map = jnp.where(slot_map > 0, slot_map + offset, -1)
    slot_map = slot_map.transpose(0, 3, 1, 2).reshape(quads, blocks * ROWS)
    token_of = jnp.arange(QUAD * tokens, dtype=jnp.int32)
    pick = (slot_map[:, :, None] == token_of[None, None, :]).astype(jnp.bfloat16)
    spread = (slot_map[:, None, :] == token_of[None, :, None]).astype(jnp.bfloat16)
    got_teacher = got[:, :bucket].reshape(devices, C, blocks, BLOCK)
    joint = 2 if turn % 2 == 0 else 1
    got_teacher = got_teacher.reshape(pairs, 2 * ROWS, blocks // joint, joint, BLOCK)
    got_teacher = got_teacher.transpose(2, 0, 3, 1, 4).reshape(blocks * per_block, BLOCK)

    once = pl.Buffered(1)
    x_rows = blocks * 2 * ROWS
    part = max(n for n in range(1, 17) if blocks % n == 0 and (n * ROWS) % 16 == 0)
    placed = []
    for pair in range(pairs):
        if ring and pair == pairs - 1:
            circle.finish(*placed)
        layout, operands = [], []
        for quad in range(2):
            two = held[pair * 4 + quad * 2 : pair * 4 + quad * 2 + 2]
            for pieces in [chip[lane] for lane in range(2) for chip in two]:
                layout.append(list(range(len(operands), len(operands) + len(pieces))))
                operands += pieces
        placed.append(
            call(
                functools.partial(place_kernel, layout),
                f"place_{pair}",
                (blocks // part,),
                [pl.BlockSpec((2, part * ROWS, QUAD * tokens), lambda s, p=pair: (p, s, 0))]
                + [pl.BlockSpec(o.shape, lambda s: (0, 0), pipeline_mode=once) for o in operands],
                pl.BlockSpec((part * 2 * ROWS, width), lambda s: (s, 0)),
                jax.ShapeDtypeStruct((x_rows, width), jnp.bfloat16),
                2 * x_rows * QUAD * tokens * width,
                2 * x_rows * width * 2,
            )(pick, *operands)
        )

    lane_slots = turn * per_block
    slot_spec = pl.BlockSpec((lane_slots, BLOCK), lambda s: (s, 0))
    flat_spec = pl.BlockSpec((BLOCK, lane_slots), lambda s: (0, s))
    x_spec = pl.BlockSpec((turn * 2 * ROWS, width), lambda s: (s, 0))
    flops = 2 * blocks * per_block * BLOCK * width
    if ring:
        part_spec = pl.BlockSpec((2, 2 * tokens, width), lambda s: (0, 0, 0), pipeline_mode=once)
        part_shape = jax.ShapeDtypeStruct((2, 2 * tokens, width), jnp.bfloat16)
        out_specs = [
            pl.BlockSpec((quads, QUAD * tokens, BLOCK), lambda s: (0, 0, 0), pipeline_mode=once)
        ] + [part_spec] * (2 * pairs)
        out_shapes = [
            jax.ShapeDtypeStruct((quads, QUAD * tokens, BLOCK), jnp.float32)
        ] + [part_shape] * (2 * pairs)
        scratch = [
            pltpu.VMEM((blocks, per_block, width), jnp.float32),
            pltpu.VMEM((blocks, per_block, BLOCK), jnp.float32),
        ]
    else:
        out_specs = [
            pl.BlockSpec((turn, per_block, columns), lambda s: (s, 0, 0))
            for columns in (width, BLOCK)
        ]
        out_shapes = [
            jax.ShapeDtypeStruct((blocks, per_block, width), jnp.bfloat16),
            jax.ShapeDtypeStruct((blocks, per_block, BLOCK), jnp.float32),
        ]
        scratch = []
    grad, *results = call(
        functools.partial(main_kernel, turn, steps, pairs, ring),
        "logits_and_back",
        (steps,),
        [
            pl.BlockSpec(memory_space=pltpu.SMEM),
            pl.BlockSpec((turn * BLOCK, width), lambda s: (s, 0)),
            slot_spec,
            pl.BlockSpec(
                spread.shape if ring else (1, 8, LANES), lambda s: (0, 0, 0), pipeline_mode=once
            ),
        ]
        + [x_spec] * pairs,
        [flat_spec] + out_specs,
        [jax.ShapeDtypeStruct((BLOCK, blocks * per_block), jnp.bfloat16)] + out_shapes,
        16 * flops,
        head.size * 2 + pairs * x_rows * width * 2,
        scratch,
    )(
        scale.reshape(1),
        head,
        got_teacher,
        spread if ring else jnp.zeros((1, 8, LANES), spread.dtype),
        *placed,
    )
    if ring:
        loss, *parts = results
    else:
        totals = []
        for value in results:
            value = value.astype(jnp.bfloat16).reshape(blocks, quads, ROWS, value.shape[-1])
            value = value.swapaxes(0, 1).reshape(quads, blocks * ROWS, value.shape[-1])
            totals.append(
                jnp.einsum("qts,qsd->qtd", spread, value, preferred_element_type=jnp.float32)
            )
        loss = totals[1]
        total = totals[0].astype(jnp.bfloat16).reshape(pairs, 2, 2, 2 * tokens, width)
        parts = [total[pair, :, lane] for lane in range(2) for pair in range(pairs)]
    own_parts, other_parts = [], []
    for pair in range(pairs):
        own_parts.append(parts[pair].reshape(4, tokens, width))
        swapped = lax.ppermute(parts[pairs + pair], "core", [(0, 1), (1, 0)])
        other_parts.append(swapped.reshape(4, tokens, width))

    lots = max(n for n in range(1, 6) if steps % n == 0)
    lot = steps // lots
    splits = 2 if turn % 4 == 0 else 1
    filled = []

    def fill(number, behind):
        shift = number * lot
        specs = [pl.BlockSpec((BLOCK, lane_slots), lambda s, d=shift: (0, s // splits + d))]
        specs += [
            pl.BlockSpec((turn * 2 * ROWS, width), lambda s, d=shift: (s // splits + d, 0))
        ] * pairs
        operands = [grad if behind is None else after(grad, behind), *placed]
        aliases = {}
        if filled:
            specs.append(pl.BlockSpec(memory_space=pl.ANY))
            aliases = {len(operands): 0}
            operands.append(filled[-1])
        out, mark = call(
            functools.partial(head_kernel, turn, splits, pairs),
            f"head_grad_{number}",
            (lot * splits,),
            specs,
            [
                pl.BlockSpec(
                    (turn // splits * BLOCK, width), lambda s, d=shift: (s + d * splits, 0)
                ),
                pl.BlockSpec((8, LANES), lambda s: (0, 0)),
            ],
            [
                jax.ShapeDtypeStruct(head.shape, jnp.bfloat16),
                jax.ShapeDtypeStruct((8, LANES), jnp.float32),
            ],
            turn * flops // lots,
            (head.size + pairs * x_rows * width) * 2 // lots,
            aliases=aliases,
        )(*operands)
        filled.append(out)
        return mark

    if ring:
        index_of = {int(o) % chips: n for n, o in enumerate(offsets)}
        half = width // 2
        sums, mark = [], None
        for step in range(1, chips + 1):
            operands, specs = [], []
            for source in (own_parts, other_parts):
                for way in range(2):
                    at = index_of[(-step, step)[way] % chips]
                    operands.append(source[at // 4])
                    specs.append(
                        pl.BlockSpec((1, tokens, half), lambda s, a=at % 4, w=way: (a, 0, w))
                    )
            for way in range(len(sums)):
                moved = lax.ppermute(sums[way], CHIPS, circle.ways[way])
                operands.append(moved if mark is None else after(moved, mark))
                specs.append(pl.BlockSpec((tokens, half), lambda s: (0, 0)))
            sums = call(
                add_kernel,
                f"ring_sum_{step}",
                (1,),
                specs,
                [pl.BlockSpec((tokens, half), lambda s: (0, 0))] * 2,
                [jax.ShapeDtypeStruct((tokens, half), jnp.bfloat16)] * 2,
                len(operands) * tokens * half,
                len(operands) * tokens * half * 2,
            )(*operands)
            mark = fill(step - 1, sums[1]) if step <= lots else None
            if step == chips - 2:
                loss = after(loss, sums[1])
        hidden_grad = jnp.concatenate(sums, axis=1)
        for number in range(min(lots, chips), lots):
            fill(number, None)
    else:
        total = [
            (own.astype(jnp.float32) + other.astype(jnp.float32)).astype(jnp.bfloat16)
            for own, other in zip(own_parts, other_parts)
        ]
        total = jnp.concatenate(total, axis=0).reshape(chips * tokens, width)
        hidden_grad = lax.psum_scatter(total, CHIPS, tiled=True)
        for number in range(lots):
            fill(number, None)
    head_grad = filled[-1]

    loss = loss[:, :, 0].reshape(devices, tokens)
    inverse = jnp.zeros((devices,), jnp.int32).at[source_of].set(jnp.arange(devices))
    loss = jnp.take(loss, inverse, axis=0)
    loss = lax.all_to_all(loss, ALL, split_axis=0, concat_axis=0, tiled=True)
    token_loss = jnp.sum(loss, axis=0)
    return hidden_grad, head_grad, token_loss


def solution(mesh):
    groups, tok, voc = (mesh.shape[name] for name in ("groups", "tok", "voc"))
    cores = Mesh(mesh.devices.reshape(groups, tok // 2, 2, voc), ("groups", "x", "core", "voc"))
    tokens_on = ("groups",) + ALL
    return jax.shard_map(
        on_device,
        mesh=cores,
        in_specs=(
            P(tokens_on, None),
            P(ALL, None),
            P(tokens_on, None),
            P(tokens_on),
            P(tokens_on, None, None),
        ),
        out_specs=(P(tokens_on, None), P(tokens_on, None), P(tokens_on)),
        check_vma=False,
    )
```

```python
import functools

import jax
import jax.numpy as jnp
import numpy as np
from jax import lax
from jax.experimental import pallas as pl
from jax.experimental.pallas import tpu as pltpu
from jax.sharding import Mesh
from jax.sharding import PartitionSpec as P

BLOCK = 128
LANES = 128
C = 2
QUAD = 4
ROWS = QUAD * C
COLS = 256
ALL = ("x", "core", "voc")
CHIPS = ("x", "voc")
RING_MOST = 8
VMEM_LIMIT = 52 * 1024 * 1024
NT = (((1,), (1,)), ((), ()))


def call(kernel, name, grid, ins, outs, shapes, flops, moved, scratch=(), aliases=None):
    return pl.pallas_call(
        kernel,
        grid=grid,
        in_specs=ins,
        out_specs=outs,
        out_shape=shapes,
        scratch_shapes=scratch,
        input_output_aliases=aliases or {},
        compiler_params=pltpu.CompilerParams(
            dimension_semantics=("arbitrary",) * len(grid), vmem_limit_bytes=VMEM_LIMIT
        ),
        cost_estimate=pl.CostEstimate(flops=flops, bytes_accessed=moved, transcendentals=0),
        name=name,
    )


def place_kernel(layout, pick_ref, *refs):
    *held, out_ref = refs
    width = out_ref.shape[1]
    blocks = out_ref.shape[0] // (2 * ROWS)
    for start in range(0, width, COLS):
        quads = []
        for quad in range(2):
            values = []
            for pieces in layout[quad * QUAD : (quad + 1) * QUAD]:
                at = start
                for number in pieces:
                    if at < held[number].shape[1]:
                        values.append(held[number][:, at : at + COLS])
                        break
                    at -= held[number].shape[1]
            rows = jnp.dot(
                pick_ref[quad], jnp.concatenate(values, axis=0), preferred_element_type=jnp.float32
            )
            quads.append(rows.reshape(blocks, ROWS, COLS))
        both = jnp.concatenate(quads, axis=1).reshape(blocks * 2 * ROWS, COLS)
        out_ref[:, start : start + COLS] = both.astype(jnp.bfloat16)


def in_block(shape, axis, pairs, joint):
    slot = lax.broadcasted_iota(jnp.int32, shape, axis)
    group = pairs * joint * 2 * ROWS
    return slot // group * joint + slot % (joint * 2 * ROWS) // (2 * ROWS)


def joint_rows(x_refs, first, joint, columns=slice(None)):
    rows = slice(first * 2 * ROWS, (first + joint) * 2 * ROWS)
    return [ref[rows, columns] for ref in x_refs]


def sum_quad(spread, rows_ref, quad, columns):
    blocks = rows_ref.shape[0]
    rows = rows_ref[:, quad * ROWS : (quad + 1) * ROWS, columns]
    rows = rows.reshape(blocks * ROWS, rows.shape[-1]).astype(jnp.bfloat16)
    return jnp.dot(spread, rows, preferred_element_type=jnp.float32)


def main_kernel(turn, steps, pairs, sums, scale_ref, head_ref, teacher_ref, map_ref, *refs):
    x_refs = refs[:pairs]
    grad_ref, *loss_ref = refs[pairs:-2]
    rows_ref, slot_loss_ref = refs[-2:]
    step = pl.program_id(0)
    origin = step * turn if sums else 0
    scale = scale_ref[0]
    joint = 2 if turn % 2 == 0 else 1
    group = pairs * joint * 2 * ROWS
    own_block = in_block((group, BLOCK), 0, pairs, joint)
    logits = []
    for first in range(0, turn, joint):
        product = lax.dot_general(
            jnp.concatenate(joint_rows(x_refs, first, joint), axis=0),
            head_ref[first * BLOCK : (first + joint) * BLOCK, :],
            NT,
            preferred_element_type=jnp.float32,
        )
        part = product[:, :BLOCK]
        for k in range(1, joint):
            part = jnp.where(own_block == k, product[:, k * BLOCK : (k + 1) * BLOCK], part)
        logits.append(part)
    logits = jnp.concatenate(logits, axis=0)

    def log_softmax(values):
        top = jnp.max(values, axis=-1, keepdims=True)
        return values - top - jnp.log(jnp.sum(jnp.exp(values - top), axis=-1, keepdims=True))

    student_log = log_softmax(logits)
    teacher_log = log_softmax(teacher_ref[...].astype(jnp.float32))
    teacher_prob = jnp.exp(teacher_log)
    loss = scale * jnp.sum(teacher_prob * (teacher_log - student_log), axis=-1, keepdims=True)
    loss = jnp.broadcast_to(loss, logits.shape)
    grad = BLOCK * scale * (jnp.exp(student_log) - teacher_prob)
    grad_ref[...] = grad.T.astype(jnp.bfloat16)
    grad = grad.astype(jnp.bfloat16)

    for first in range(0, turn, joint):
        here = slice(first * pairs * 2 * ROWS, (first + joint) * pairs * 2 * ROWS)
        lines = [
            jnp.where(own_block == k, grad[here], jnp.zeros_like(grad[here])) for k in range(joint)
        ]
        grads = jnp.dot(
            jnp.concatenate(lines, axis=1),
            head_ref[first * BLOCK : (first + joint) * BLOCK, :],
            preferred_element_type=jnp.float32,
        )
        for pair in range(pairs):
            to = slice(pair * 2 * ROWS, (pair + 1) * 2 * ROWS)
            for k in range(joint):
                start = (pair * joint + k) * 2 * ROWS
                rows_ref[origin + first + k, to, :] = grads[start : start + 2 * ROWS].astype(
                    rows_ref.dtype
                )
                start += here.start
                slot_loss_ref[origin + first + k, to, :] = loss[start : start + 2 * ROWS]

    if not sums:
        return
    loss_ref, *part_refs = loss_ref

    @pl.when(step == steps - 1)
    def _():
        quad_tokens = loss_ref.shape[1]
        half = quad_tokens // 2
        for quad in range(2 * pairs):
            slots = map_ref[quad : quad + 1, :]
            token = lax.broadcasted_iota(jnp.int32, (quad_tokens, slots.shape[1]), 0)
            spread = jnp.where(slots == token, 1.0, 0.0).astype(jnp.bfloat16)
            loss_ref[quad] = sum_quad(spread, slot_loss_ref, quad, slice(0, BLOCK))
            for start in range(0, rows_ref.shape[-1], COLS):
                columns = slice(start, start + COLS)
                total = sum_quad(spread, rows_ref, quad, columns).astype(jnp.bfloat16)
                part_refs[quad // 2][quad % 2, :, columns] = total[:half]
                part_refs[pairs + quad // 2][quad % 2, :, columns] = total[half:]


def head_kernel(turn, splits, pairs, grad_ref, *refs):
    x_refs, (out_ref, mark_ref) = refs[:pairs], refs[-2:]
    joint = 2 if turn % 2 == 0 else 1
    slots = grad_ref.shape[1]
    share = turn // splits
    place = in_block((1, slots), 1, pairs, joint) - pl.program_id(0) % splits * share
    grad = grad_ref[...]
    spaced = [grad * (place == index).astype(jnp.bfloat16) for index in range(share)]
    spaced = jnp.concatenate(spaced, axis=0)
    for start in range(0, out_ref.shape[1], COLS):
        columns = slice(start, start + COLS)
        rows = [
            piece
            for first in range(0, turn, joint)
            for piece in joint_rows(x_refs, first, joint, columns)
        ]
        out_ref[:, columns] = jnp.dot(
            spaced, jnp.concatenate(rows, axis=0), preferred_element_type=jnp.float32
        ).astype(jnp.bfloat16)
    mark_ref[...] = jnp.zeros_like(mark_ref)


def add_kernel(*refs):
    *terms, right_ref, left_ref = refs
    for way, out_ref in enumerate((right_ref, left_ref)):
        total = sum(ref[...].reshape(out_ref.shape).astype(jnp.float32) for ref in terms[way::2])
        out_ref[...] = total.astype(jnp.bfloat16)


def ring_order(rows, columns):
    order = []
    for r in range(rows):
        line = [r * columns + c for c in range(columns)]
        order += line if r % 2 == 0 else line[::-1]
    return order


def arrivals(chips):
    near = [0]
    for step in range(1, chips // 2):
        near += [-step, step]
    return near + [chips // 2]


def after(value, *others):
    return lax.optimization_barrier((value, *others))[0]


class Ring:
    def __init__(self, hidden, order):
        chips = len(order)
        half = hidden.shape[1] // 2
        self.ways = [
            [(order[p], order[(p + way) % chips]) for p in range(chips)] for way in (1, -1)
        ]
        halves = [hidden[:, :half], hidden[:, half:]]
        self.moving = [halves, halves]
        self.got = [self.both(halves)]

    def both(self, pieces):
        return pieces, [lax.ppermute(piece, "core", [(0, 1), (1, 0)]) for piece in pieces]

    def step(self):
        self.moving = [
            [lax.ppermute(piece, CHIPS, way) for piece in pieces]
            for pieces, way in zip(self.moving, self.ways)
        ]
        self.got += [self.both(pieces) for pieces in self.moving]

    def last(self, *behind):
        pieces = [after(self.moving[way][way], *behind) for way in range(2)]
        self.got += [self.both([lax.ppermute(p, CHIPS, w) for p, w in zip(pieces, self.ways)])]


def gather_whole(hidden):
    chips = lax.axis_size(CHIPS)
    own = lax.all_gather(hidden, CHIPS, axis=0)
    other = lax.ppermute(own, "core", [(0, 1), (1, 0)])
    return [([own[chip]], [other[chip]]) for chip in range(chips)]


def on_device(hidden, head, block_ids, live_counts, teacher):
    across, down = lax.axis_size("x"), lax.axis_size("voc")
    chips = across * down
    devices = 2 * chips
    pairs = chips // 4
    tokens, list_width = block_ids.shape
    width = hidden.shape[1]
    blocks = head.shape[0] // BLOCK
    even = [n for n in range(2, 9, 2) if blocks % n == 0]
    turn = max(even) if even else 1
    steps = blocks // turn
    entries = tokens * list_width
    bucket = blocks * C
    per_block = devices * C
    core = lax.axis_index("core")
    ring = chips <= RING_MOST
    order = ring_order(across, down)
    if ring:
        circle = Ring(hidden, order)
        for _ in range(chips // 2 - 1):
            circle.step()
        held = circle.got
        offsets = np.array(arrivals(chips))
        places = np.argsort(np.array(order))
        spot = jnp.asarray(places, jnp.int32)[lax.axis_index(CHIPS)]
        chip_of = jnp.asarray(np.array(order), jnp.int32)[(spot + offsets) % chips]
    else:
        held = gather_whole(hidden)
        offsets = np.arange(chips)
        chip_of = jnp.arange(chips, dtype=jnp.int32)

    flat_ids = block_ids.reshape(entries)
    position = jnp.arange(entries, dtype=jnp.int32)
    earlier = (flat_ids[:, None] == flat_ids[None, :]) & (position[:, None] > position[None, :])
    ranks = jnp.sum(earlier, axis=1, dtype=jnp.int32)
    live = (jnp.arange(list_width, dtype=jnp.int32)[None, :] < live_counts[:, None]).reshape(entries)
    map_rows = -(-bucket // BLOCK)
    meta_at = -(-bucket // 16) * 16
    deep = meta_at + -(-(map_rows + 2) // 16) * 16
    rows = flat_ids // blocks * deep + ranks * blocks + flat_ids % blocks
    slots = jnp.arange(devices * deep, dtype=jnp.int32)
    place = (slots[:, None] == rows[None, :]).astype(jnp.bfloat16)
    send_teacher = jnp.dot(
        place, teacher.reshape(entries, BLOCK), preferred_element_type=jnp.float32
    ).astype(jnp.bfloat16)
    named = jnp.where(live, position // list_width + 1, 0)
    tight = flat_ids // blocks * bucket + ranks * blocks + flat_ids % blocks
    spots = jnp.arange(devices * bucket, dtype=jnp.int32)
    send_map = jnp.sum(jnp.where(tight[:, None] == spots[None, :], named[:, None], 0), axis=0)
    send_map = send_map.reshape(devices, bucket)
    send_map = jnp.pad(send_map, ((0, 0), (0, map_rows * BLOCK - bucket)))
    live_sum = jnp.sum(live_counts)
    send_meta = jnp.concatenate(
        [
            send_map.reshape(devices, map_rows, BLOCK),
            jnp.broadcast_to(live_sum // 256, (devices, 1, BLOCK)),
            jnp.broadcast_to(live_sum % 256, (devices, 1, BLOCK)),
            jnp.zeros((devices, deep - meta_at - map_rows - 2, BLOCK), jnp.int32),
        ],
        axis=1,
    ).astype(jnp.bfloat16)
    sent = lax.dynamic_update_slice(
        send_teacher.reshape(devices, deep, BLOCK), send_meta, (0, meta_at, 0)
    )
    got = lax.all_to_all(sent, ALL, split_axis=0, concat_axis=0, tiled=True)

    lanes = jnp.stack([core, 1 - core])
    pair_of = chip_of.reshape(chips // 2, 1, 2)
    source_of = (pair_of // down * 2 + lanes[None, :, None]) * down + pair_of % down
    source_of = source_of.reshape(devices)
    got = got.at[source_of].get(mode="promise_in_bounds")
    meta = got[:, meta_at:].astype(jnp.int32)
    live_total = jnp.sum(meta[:, map_rows, 0] * 256 + meta[:, map_rows + 1, 0])
    scale = jnp.float32(tokens * devices) / live_total.astype(jnp.float32)
    slot_map = meta[:, :map_rows].reshape(devices, map_rows * BLOCK)[:, :bucket]
    quads = devices // QUAD
    slot_map = slot_map.reshape(quads, ROWS, blocks)
    offset = jnp.arange(ROWS, dtype=jnp.int32)[None, :, None] // C * tokens - 1
    slot_map = jnp.where(slot_map > 0, slot_map + offset, -1)
    slot_map = slot_map.swapaxes(1, 2).reshape(quads, blocks * ROWS)
    token_of = jnp.arange(QUAD * tokens, dtype=jnp.int32)
    pick = (slot_map[:, :, None] == token_of[None, None, :]).astype(jnp.bfloat16)
    got_teacher = got[:, :bucket].reshape(devices, C, blocks, BLOCK)
    joint = 2 if turn % 2 == 0 else 1
    got_teacher = got_teacher.reshape(pairs, 2 * ROWS, blocks // joint, joint, BLOCK)
    got_teacher = got_teacher.transpose(2, 0, 3, 1, 4).reshape(blocks * per_block, BLOCK)

    once = pl.Buffered(1)
    x_rows = blocks * 2 * ROWS
    part = max(n for n in range(1, 17) if blocks % n == 0 and (n * ROWS) % 16 == 0)
    placed = []
    for pair in range(pairs):
        if ring and pair == pairs - 1:
            circle.last(*placed)
        layout, operands = [], []
        for quad in range(2):
            two = held[pair * 4 + quad * 2 : pair * 4 + quad * 2 + 2]
            for pieces in [chip[lane] for lane in range(2) for chip in two]:
                layout.append(list(range(len(operands), len(operands) + len(pieces))))
                operands += pieces
        placed.append(
            call(
                functools.partial(place_kernel, layout),
                f"place_{pair}",
                (blocks // part,),
                [pl.BlockSpec((2, part * ROWS, QUAD * tokens), lambda s, p=pair: (p, s, 0))]
                + [pl.BlockSpec(o.shape, lambda s: (0, 0), pipeline_mode=once) for o in operands],
                pl.BlockSpec((part * 2 * ROWS, width), lambda s: (s, 0)),
                jax.ShapeDtypeStruct((x_rows, width), jnp.bfloat16),
                2 * x_rows * QUAD * tokens * width,
                2 * x_rows * width * 2,
            )(pick, *operands)
        )

    lane_slots = turn * per_block
    slot_spec = pl.BlockSpec((lane_slots, BLOCK), lambda s: (s, 0))
    flat_spec = pl.BlockSpec((BLOCK, lane_slots), lambda s: (0, s))
    x_spec = pl.BlockSpec((turn * 2 * ROWS, width), lambda s: (s, 0))
    flops = 2 * blocks * per_block * BLOCK * width
    if ring:
        part_spec = pl.BlockSpec((2, 2 * tokens, width), lambda s: (0, 0, 0), pipeline_mode=once)
        part_shape = jax.ShapeDtypeStruct((2, 2 * tokens, width), jnp.bfloat16)
        out_specs = [
            pl.BlockSpec((quads, QUAD * tokens, BLOCK), lambda s: (0, 0, 0), pipeline_mode=once)
        ] + [part_spec] * (2 * pairs)
        out_shapes = [
            jax.ShapeDtypeStruct((quads, QUAD * tokens, BLOCK), jnp.float32)
        ] + [part_shape] * (2 * pairs)
        scratch = [
            pltpu.VMEM((blocks, per_block, width), jnp.float32),
            pltpu.VMEM((blocks, per_block, BLOCK), jnp.float32),
        ]
    else:
        out_specs = [
            pl.BlockSpec((turn, per_block, columns), lambda s: (s, 0, 0))
            for columns in (width, BLOCK)
        ]
        out_shapes = [
            jax.ShapeDtypeStruct((blocks, per_block, width), jnp.bfloat16),
            jax.ShapeDtypeStruct((blocks, per_block, BLOCK), jnp.float32),
        ]
        scratch = []
    grad, *results = call(
        functools.partial(main_kernel, turn, steps, pairs, ring),
        "logits_and_back",
        (steps,),
        [
            pl.BlockSpec(memory_space=pltpu.SMEM),
            pl.BlockSpec((turn * BLOCK, width), lambda s: (s, 0)),
            slot_spec,
            pl.BlockSpec(slot_map.shape, lambda s: (0, 0), pipeline_mode=once),
        ]
        + [x_spec] * pairs,
        [flat_spec] + out_specs,
        [jax.ShapeDtypeStruct((BLOCK, blocks * per_block), jnp.bfloat16)] + out_shapes,
        16 * flops,
        head.size * 2 + pairs * x_rows * width * 2,
        scratch,
    )(
        scale.reshape(1),
        head,
        got_teacher,
        slot_map,
        *placed,
    )
    if ring:
        loss, *parts = results
    else:
        totals = []
        for value in results:
            value = value.astype(jnp.bfloat16).reshape(blocks, quads, ROWS, value.shape[-1])
            value = value.swapaxes(0, 1).reshape(quads, blocks * ROWS, value.shape[-1])
            totals.append(
                jnp.einsum("qst,qsd->qtd", pick, value, preferred_element_type=jnp.float32)
            )
        loss = totals[1]
        total = totals[0].astype(jnp.bfloat16).reshape(pairs, 2, 2, 2 * tokens, width)
        parts = [total[pair, :, lane] for lane in range(2) for pair in range(pairs)]
    own_parts, other_parts = [], []
    for pair in range(pairs):
        own_parts.append(parts[pair].reshape(4, tokens, width))
        swapped = lax.ppermute(parts[pairs + pair], "core", [(0, 1), (1, 0)])
        other_parts.append(swapped.reshape(4, tokens, width))

    inverse = jnp.sum(
        jnp.where(source_of[None, :] == jnp.arange(devices)[:, None], jnp.arange(devices)[None], 0),
        axis=1,
    )
    loss = loss[:, :, 0].reshape(devices, tokens)
    loss = loss.at[inverse].get(mode="promise_in_bounds")

    def return_loss(behind=None):
        sent = loss if behind is None else after(loss, behind)
        back = lax.all_to_all(sent, ALL, split_axis=0, concat_axis=0, tiled=True)
        return jnp.sum(back, axis=0)

    lots = max(n for n in range(1, 6) if steps % n == 0)
    lot = steps // lots
    splits = 2 if turn % 4 == 0 else 1
    filled = []

    def fill(number, behind):
        shift = number * lot
        specs = [pl.BlockSpec((BLOCK, lane_slots), lambda s, d=shift: (0, s // splits + d))]
        specs += [
            pl.BlockSpec((turn * 2 * ROWS, width), lambda s, d=shift: (s // splits + d, 0))
        ] * pairs
        operands = [grad if behind is None else after(grad, behind), *placed]
        aliases = {}
        if filled:
            specs.append(pl.BlockSpec(memory_space=pl.ANY))
            aliases = {len(operands): 0}
            operands.append(filled[-1])
        out, mark = call(
            functools.partial(head_kernel, turn, splits, pairs),
            f"head_grad_{number}",
            (lot * splits,),
            specs,
            [
                pl.BlockSpec(
                    (turn // splits * BLOCK, width), lambda s, d=shift: (s + d * splits, 0)
                ),
                pl.BlockSpec((8, LANES), lambda s: (0, 0)),
            ],
            [
                jax.ShapeDtypeStruct(head.shape, jnp.bfloat16),
                jax.ShapeDtypeStruct((8, LANES), jnp.float32),
            ],
            turn * flops // lots,
            (head.size + pairs * x_rows * width) * 2 // lots,
            aliases=aliases,
        )(*operands)
        filled.append(out)
        return mark

    if ring:
        index_of = {int(o) % chips: n for n, o in enumerate(offsets)}
        half = width // 2
        sums, mark = [], None
        for step in range(1, chips + 1):
            operands, specs = [], []
            for source in (own_parts, other_parts):
                for way in range(2):
                    at = index_of[(-step, step)[way] % chips]
                    operands.append(source[at // 4])
                    specs.append(
                        pl.BlockSpec((1, tokens, half), lambda s, a=at % 4, w=way: (a, 0, w))
                    )
            for way in range(len(sums)):
                moved = lax.ppermute(sums[way], CHIPS, circle.ways[way])
                operands.append(moved if mark is None else after(moved, mark))
                specs.append(pl.BlockSpec((tokens, half), lambda s: (0, 0)))
            sums = call(
                add_kernel,
                f"ring_sum_{step}",
                (1,),
                specs,
                [pl.BlockSpec((tokens, half), lambda s: (0, 0))] * 2,
                [jax.ShapeDtypeStruct((tokens, half), jnp.bfloat16)] * 2,
                len(operands) * tokens * half,
                len(operands) * tokens * half * 2,
            )(*operands)
            mark = fill(step - 1, sums[1]) if step <= lots else None
            if step == lots + 1:
                mark = token_loss = return_loss(sums[1])
        hidden_grad = jnp.concatenate(sums, axis=1)
    else:
        token_loss = return_loss()
        total = [
            (own.astype(jnp.float32) + other.astype(jnp.float32)).astype(jnp.bfloat16)
            for own, other in zip(own_parts, other_parts)
        ]
        total = jnp.concatenate(total, axis=0).reshape(chips * tokens, width)
        hidden_grad = lax.psum_scatter(total, CHIPS, tiled=True)
        for number in range(lots):
            fill(number, None)
    head_grad = filled[-1]

    return hidden_grad, head_grad, token_loss


def solution(mesh):
    groups, tok, voc = (mesh.shape[name] for name in ("groups", "tok", "voc"))
    cores = Mesh(mesh.devices.reshape(groups, tok // 2, 2, voc), ("groups", "x", "core", "voc"))
    tokens_on = ("groups",) + ALL
    return jax.shard_map(
        on_device,
        mesh=cores,
        in_specs=(
            P(tokens_on, None),
            P(ALL, None),
            P(tokens_on, None),
            P(tokens_on),
            P(tokens_on, None, None),
        ),
        out_specs=(P(tokens_on, None), P(tokens_on, None), P(tokens_on)),
        check_vma=False,
    )
```

```python
import functools

import jax
import jax.numpy as jnp
import numpy as np
from jax import lax
from jax.experimental import pallas as pl
from jax.experimental.pallas import tpu as pltpu
from jax.sharding import Mesh
from jax.sharding import PartitionSpec as P

BLOCK = 128
LANES = 128
C = 2
QUAD = 4
ROWS = QUAD * C
COLS = 256
ALL = ("x", "core", "voc")
CHIPS = ("x", "voc")
RING_MOST = 8
MIB = 1024 * 1024
NT = (((1,), (1,)), ((), ()))


def call(kernel, name, grid, ins, outs, shapes, flops, moved, vmem, scratch=(), aliases=None):
    return pl.pallas_call(
        kernel,
        grid=grid,
        in_specs=ins,
        out_specs=outs,
        out_shape=shapes,
        scratch_shapes=scratch,
        input_output_aliases=aliases or {},
        compiler_params=pltpu.CompilerParams(
            dimension_semantics=("arbitrary",) * len(grid), vmem_limit_bytes=vmem * MIB
        ),
        cost_estimate=pl.CostEstimate(flops=flops, bytes_accessed=moved, transcendentals=0),
        name=name,
    )


def place_kernel(layout, pick_ref, *refs):
    *held, out_ref = refs
    width = out_ref.shape[1]
    blocks = out_ref.shape[0] // (2 * ROWS)
    for start in range(0, width, COLS):
        quads = []
        for quad in range(2):
            values = []
            for pieces in layout[quad * QUAD : (quad + 1) * QUAD]:
                at = start
                for number in pieces:
                    if at < held[number].shape[1]:
                        values.append(held[number][:, at : at + COLS])
                        break
                    at -= held[number].shape[1]
            rows = jnp.dot(
                pick_ref[quad], jnp.concatenate(values, axis=0), preferred_element_type=jnp.float32
            )
            quads.append(rows.reshape(blocks, ROWS, COLS))
        both = jnp.concatenate(quads, axis=1).reshape(blocks * 2 * ROWS, COLS)
        out_ref[:, start : start + COLS] = both.astype(jnp.bfloat16)


def in_block(shape, axis, pairs, joint):
    slot = lax.broadcasted_iota(jnp.int32, shape, axis)
    group = pairs * joint * 2 * ROWS
    return slot // group * joint + slot % (joint * 2 * ROWS) // (2 * ROWS)


def joint_rows(x_refs, first, joint, columns=slice(None)):
    rows = slice(first * 2 * ROWS, (first + joint) * 2 * ROWS)
    return [ref[rows, columns] for ref in x_refs]


def sum_quad(spread, rows_ref, quad, columns):
    blocks = rows_ref.shape[0]
    rows = rows_ref[:, quad * ROWS : (quad + 1) * ROWS, columns]
    rows = rows.reshape(blocks * ROWS, rows.shape[-1]).astype(jnp.bfloat16)
    return jnp.dot(spread, rows, preferred_element_type=jnp.float32)


def two_parts(values):
    high = values.astype(jnp.bfloat16)
    low = (values - high.astype(jnp.float32)).astype(jnp.bfloat16)
    lane = lax.broadcasted_iota(jnp.int32, values.shape, 1)
    return jnp.where(lane < LANES // 2, high.astype(jnp.float32), low.astype(jnp.float32)).astype(
        jnp.bfloat16
    )


def joined(values):
    values = values.astype(jnp.float32)
    return values + pltpu.roll(values, LANES // 2, 1)


def main_kernel(turn, steps, pairs, sums, scale_ref, head_ref, teacher_ref, map_ref, *refs):
    x_refs = refs[:pairs]
    grad_ref, *loss_ref = refs[pairs:-2]
    rows_ref, slot_loss_ref = refs[-2:]
    step = pl.program_id(0)
    origin = step * turn if sums else 0
    scale = scale_ref[0]
    joint = 2 if turn % 2 == 0 else 1
    group = pairs * joint * 2 * ROWS
    own_block = in_block((group, BLOCK), 0, pairs, joint)
    logits = []
    for first in range(0, turn, joint):
        product = lax.dot_general(
            jnp.concatenate(joint_rows(x_refs, first, joint), axis=0),
            head_ref[first * BLOCK : (first + joint) * BLOCK, :],
            NT,
            preferred_element_type=jnp.float32,
        )
        part = product[:, :BLOCK]
        for k in range(1, joint):
            part = jnp.where(own_block == k, product[:, k * BLOCK : (k + 1) * BLOCK], part)
        logits.append(part)
    logits = jnp.concatenate(logits, axis=0)

    def log_softmax(values):
        top = jnp.max(values, axis=-1, keepdims=True)
        return values - top - jnp.log(jnp.sum(jnp.exp(values - top), axis=-1, keepdims=True))

    student_log = log_softmax(logits)
    teacher_log = log_softmax(teacher_ref[...].astype(jnp.float32))
    teacher_prob = jnp.exp(teacher_log)
    loss = scale * jnp.sum(teacher_prob * (teacher_log - student_log), axis=-1, keepdims=True)
    loss = jnp.broadcast_to(loss, logits.shape)
    grad = BLOCK * scale * (jnp.exp(student_log) - teacher_prob)
    grad_ref[...] = grad.T.astype(jnp.bfloat16)
    grad = grad.astype(jnp.bfloat16)

    for first in range(0, turn, joint):
        here = slice(first * pairs * 2 * ROWS, (first + joint) * pairs * 2 * ROWS)
        lines = [
            jnp.where(own_block == k, grad[here], jnp.zeros_like(grad[here])) for k in range(joint)
        ]
        grads = jnp.dot(
            jnp.concatenate(lines, axis=1),
            head_ref[first * BLOCK : (first + joint) * BLOCK, :],
            preferred_element_type=jnp.float32,
        )
        for pair in range(pairs):
            to = slice(pair * 2 * ROWS, (pair + 1) * 2 * ROWS)
            for k in range(joint):
                start = (pair * joint + k) * 2 * ROWS
                rows_ref[origin + first + k, to, :] = grads[start : start + 2 * ROWS].astype(
                    rows_ref.dtype
                )
                start += here.start
                slot_loss_ref[origin + first + k, to, :] = loss[start : start + 2 * ROWS]

    if not sums:
        return
    part_refs = loss_ref

    @pl.when(step == steps - 1)
    def _():
        half = part_refs[0].shape[1]
        width = rows_ref.shape[-1]
        for quad in range(2 * pairs):
            slots = map_ref[quad : quad + 1, :]
            token = lax.broadcasted_iota(jnp.int32, (2 * half, slots.shape[1]), 0)
            spread = jnp.where(slots == token, 1.0, 0.0).astype(jnp.bfloat16)

            def put(columns, total):
                part_refs[quad // 2][quad % 2, :, columns] = total[:half]
                part_refs[pairs + quad // 2][quad % 2, :, columns] = total[half:]

            loss = sum_quad(spread, slot_loss_ref, quad, slice(0, LANES))
            put(slice(width, width + LANES), two_parts(loss))
            for start in range(0, width, COLS):
                columns = slice(start, start + COLS)
                put(columns, sum_quad(spread, rows_ref, quad, columns).astype(jnp.bfloat16))


def head_kernel(turn, splits, shift, pairs, grad_ref, *refs):
    x_refs, (out_ref, mark_ref) = refs[:pairs], refs[-2:]
    joint = 2 if turn % 2 == 0 else 1
    slots = grad_ref.shape[1]
    share = turn // splits
    place = in_block((1, slots), 1, pairs, joint) - (pl.program_id(0) + shift) % splits * share
    grad = grad_ref[...]
    spaced = [grad * (place == index).astype(jnp.bfloat16) for index in range(share)]
    spaced = jnp.concatenate(spaced, axis=0)
    for start in range(0, out_ref.shape[1], COLS):
        columns = slice(start, start + COLS)
        rows = [
            piece
            for first in range(0, turn, joint)
            for piece in joint_rows(x_refs, first, joint, columns)
        ]
        out_ref[:, columns] = jnp.dot(
            spaced, jnp.concatenate(rows, axis=0), preferred_element_type=jnp.float32
        ).astype(jnp.bfloat16)
    mark_ref[...] = jnp.zeros_like(mark_ref)


def add_kernel(last, *refs):
    own_right, own_left, own_loss, other_right, other_left, other_loss = refs[:6]
    half = own_right.shape[-1]
    moved, outs = (refs[6:], ()) if len(refs) == 8 else (refs[6:8], refs[8:])
    moved, outs = (moved, outs) if outs else ((), moved)

    def whole(ref):
        return ref[...].reshape(ref.shape[-2:]).astype(jnp.float32)

    right = whole(own_right) + whole(other_right)
    left = whole(own_left) + whole(other_left)
    loss = joined(whole(own_loss)) + joined(whole(other_loss))
    if moved:
        right += moved[0][:, :half].astype(jnp.float32)
        left += moved[1][...].astype(jnp.float32)
        loss += joined(moved[0][:, half:])
    if last:
        outs[0][:, :half] = right.astype(jnp.bfloat16)
        outs[0][:, half:] = left.astype(jnp.bfloat16)
        outs[1][...] = loss
    else:
        outs[0][:, :half] = right.astype(jnp.bfloat16)
        outs[0][:, half:] = two_parts(loss)
        outs[1][...] = left.astype(jnp.bfloat16)


def ring_order(rows, columns):
    order = []
    for r in range(rows):
        line = [r * columns + c for c in range(columns)]
        order += line if r % 2 == 0 else line[::-1]
    return order


def arrivals(chips):
    near = [0]
    for step in range(1, chips // 2):
        near += [-step, step]
    return near + [chips // 2]


def after(value, *others):
    return lax.optimization_barrier((value, *others))[0]


class Ring:
    def __init__(self, hidden, order):
        chips = len(order)
        half = hidden.shape[1] // 2
        self.ways = [
            [(order[p], order[(p + way) % chips]) for p in range(chips)] for way in (1, -1)
        ]
        halves = [hidden[:, :half], hidden[:, half:]]
        self.moving = [halves, halves]
        self.got = [self.both(halves)]

    def both(self, pieces):
        return pieces, [lax.ppermute(piece, "core", [(0, 1), (1, 0)]) for piece in pieces]

    def step(self):
        self.moving = [
            [lax.ppermute(piece, CHIPS, way) for piece in pieces]
            for pieces, way in zip(self.moving, self.ways)
        ]
        self.got += [self.both(pieces) for pieces in self.moving]

    def last(self, *behind):
        pieces = [after(self.moving[way][way], *behind) for way in range(2)]
        self.got += [self.both([lax.ppermute(p, CHIPS, w) for p, w in zip(pieces, self.ways)])]


def gather_whole(hidden):
    chips = lax.axis_size(CHIPS)
    own = lax.all_gather(hidden, CHIPS, axis=0)
    other = lax.ppermute(own, "core", [(0, 1), (1, 0)])
    return [([own[chip]], [other[chip]]) for chip in range(chips)]


def on_device(hidden, head, block_ids, live_counts, teacher):
    across, down = lax.axis_size("x"), lax.axis_size("voc")
    chips = across * down
    devices = 2 * chips
    pairs = chips // 4
    tokens, list_width = block_ids.shape
    width = hidden.shape[1]
    blocks = head.shape[0] // BLOCK
    even = [n for n in range(2, 9, 2) if blocks % n == 0]
    turn = max(even) if even else 1
    steps = blocks // turn
    entries = tokens * list_width
    bucket = blocks * C
    per_block = devices * C
    core = lax.axis_index("core")
    ring = chips <= RING_MOST
    order = ring_order(across, down)
    if ring:
        circle = Ring(hidden, order)
        for _ in range(chips // 2 - 1):
            circle.step()
        held = circle.got
        offsets = np.array(arrivals(chips))
        places = np.argsort(np.array(order))
        spot = jnp.asarray(places, jnp.int32)[lax.axis_index(CHIPS)]
        chip_of = jnp.asarray(np.array(order), jnp.int32)[(spot + offsets) % chips]
    else:
        held = gather_whole(hidden)
        offsets = np.arange(chips)
        chip_of = jnp.arange(chips, dtype=jnp.int32)

    flat_ids = block_ids.reshape(entries)
    position = jnp.arange(entries, dtype=jnp.int32)
    earlier = (flat_ids[:, None] == flat_ids[None, :]) & (position[:, None] > position[None, :])
    ranks = jnp.sum(earlier, axis=1, dtype=jnp.int32)
    live = (jnp.arange(list_width, dtype=jnp.int32)[None, :] < live_counts[:, None]).reshape(entries)
    map_rows = -(-bucket // BLOCK)
    meta_at = -(-bucket // 16) * 16
    deep = meta_at + -(-(map_rows + 2) // 16) * 16
    rows = flat_ids // blocks * deep + ranks * blocks + flat_ids % blocks
    slots = jnp.arange(devices * deep, dtype=jnp.int32)
    place = (slots[:, None] == rows[None, :]).astype(jnp.bfloat16)
    send_teacher = jnp.dot(
        place, teacher.reshape(entries, BLOCK), preferred_element_type=jnp.float32
    ).astype(jnp.bfloat16)
    named = jnp.where(live, position // list_width + 1, 0)
    tight = flat_ids // blocks * bucket + ranks * blocks + flat_ids % blocks
    spots = jnp.arange(devices * bucket, dtype=jnp.int32)
    send_map = jnp.sum(jnp.where(tight[:, None] == spots[None, :], named[:, None], 0), axis=0)
    send_map = send_map.reshape(devices, bucket)
    send_map = jnp.pad(send_map, ((0, 0), (0, map_rows * BLOCK - bucket)))
    live_sum = jnp.sum(live_counts)
    send_meta = jnp.concatenate(
        [
            send_map.reshape(devices, map_rows, BLOCK),
            jnp.broadcast_to(live_sum // 256, (devices, 1, BLOCK)),
            jnp.broadcast_to(live_sum % 256, (devices, 1, BLOCK)),
            jnp.zeros((devices, deep - meta_at - map_rows - 2, BLOCK), jnp.int32),
        ],
        axis=1,
    ).astype(jnp.bfloat16)
    sent = lax.dynamic_update_slice(
        send_teacher.reshape(devices, deep, BLOCK), send_meta, (0, meta_at, 0)
    )
    if ring:
        sent = after(sent, *held[1][0], *held[2][0])
    got = lax.all_to_all(sent, ALL, split_axis=0, concat_axis=0, tiled=True)

    lanes = jnp.stack([core, 1 - core])
    pair_of = chip_of.reshape(chips // 2, 1, 2)
    source_of = (pair_of // down * 2 + lanes[None, :, None]) * down + pair_of % down
    source_of = source_of.reshape(devices)
    got = got.at[source_of].get(mode="promise_in_bounds")
    meta = got[:, meta_at:].astype(jnp.int32)
    live_total = jnp.sum(meta[:, map_rows, 0] * 256 + meta[:, map_rows + 1, 0])
    scale = jnp.float32(tokens * devices) / live_total.astype(jnp.float32)
    slot_map = meta[:, :map_rows].reshape(devices, map_rows * BLOCK)[:, :bucket]
    quads = devices // QUAD
    slot_map = slot_map.reshape(quads, ROWS, blocks)
    offset = jnp.arange(ROWS, dtype=jnp.int32)[None, :, None] // C * tokens - 1
    slot_map = jnp.where(slot_map > 0, slot_map + offset, -1)
    slot_map = slot_map.swapaxes(1, 2).reshape(quads, blocks * ROWS)
    token_of = jnp.arange(QUAD * tokens, dtype=jnp.int32)
    pick = (slot_map[:, :, None] == token_of[None, None, :]).astype(jnp.bfloat16)
    got_teacher = got[:, :bucket].reshape(devices, C, blocks, BLOCK)
    joint = 2 if turn % 2 == 0 else 1
    got_teacher = got_teacher.reshape(pairs, 2 * ROWS, blocks // joint, joint, BLOCK)
    got_teacher = got_teacher.transpose(2, 0, 3, 1, 4).reshape(blocks * per_block, BLOCK)

    once = pl.Buffered(1)
    x_rows = blocks * 2 * ROWS
    part = max(n for n in range(1, 17) if blocks % n == 0 and (n * ROWS) % 16 == 0)
    placed = []
    for pair in range(pairs):
        if ring and pair == pairs - 1:
            circle.last(*placed)
        layout, operands = [], []
        for quad in range(2):
            two = held[pair * 4 + quad * 2 : pair * 4 + quad * 2 + 2]
            for pieces in [chip[lane] for lane in range(2) for chip in two]:
                layout.append(list(range(len(operands), len(operands) + len(pieces))))
                operands += pieces
        placed.append(
            call(
                functools.partial(place_kernel, layout),
                f"place_{pair}",
                (blocks // part,),
                [pl.BlockSpec((2, part * ROWS, QUAD * tokens), lambda s, p=pair: (p, s, 0))]
                + [pl.BlockSpec(o.shape, lambda s: (0, 0), pipeline_mode=once) for o in operands],
                pl.BlockSpec((part * 2 * ROWS, width), lambda s: (s, 0)),
                jax.ShapeDtypeStruct((x_rows, width), jnp.bfloat16),
                2 * x_rows * QUAD * tokens * width,
                2 * x_rows * width * 2,
                28,
            )(pick, *operands)
        )

    lane_slots = turn * per_block
    slot_spec = pl.BlockSpec((lane_slots, BLOCK), lambda s: (s, 0))
    flat_spec = pl.BlockSpec((BLOCK, lane_slots), lambda s: (0, s))
    x_spec = pl.BlockSpec((turn * 2 * ROWS, width), lambda s: (s, 0))
    flops = 2 * blocks * per_block * BLOCK * width
    if ring:
        part = (2, 2 * tokens, width + LANES)
        out_specs = [pl.BlockSpec(part, lambda s: (0, 0, 0), pipeline_mode=once)] * (2 * pairs)
        out_shapes = [jax.ShapeDtypeStruct(part, jnp.bfloat16)] * (2 * pairs)
        scratch = [
            pltpu.VMEM((blocks, per_block, width), jnp.float32),
            pltpu.VMEM((blocks, per_block, BLOCK), jnp.float32),
        ]
    else:
        out_specs = [
            pl.BlockSpec((turn, per_block, columns), lambda s: (s, 0, 0))
            for columns in (width, BLOCK)
        ]
        out_shapes = [
            jax.ShapeDtypeStruct((blocks, per_block, width), jnp.bfloat16),
            jax.ShapeDtypeStruct((blocks, per_block, BLOCK), jnp.float32),
        ]
        scratch = []
    grad, *results = call(
        functools.partial(main_kernel, turn, steps, pairs, ring),
        "logits_and_back",
        (steps,),
        [
            pl.BlockSpec(memory_space=pltpu.SMEM),
            pl.BlockSpec((turn * BLOCK, width), lambda s: (s, 0)),
            slot_spec,
            pl.BlockSpec(slot_map.shape, lambda s: (0, 0), pipeline_mode=once),
        ]
        + [x_spec] * pairs,
        [flat_spec] + out_specs,
        [jax.ShapeDtypeStruct((BLOCK, blocks * per_block), jnp.bfloat16)] + out_shapes,
        16 * flops,
        head.size * 2 + pairs * x_rows * width * 2,
        52,
        scratch,
    )(
        scale.reshape(1),
        head,
        got_teacher,
        slot_map,
        *placed,
    )
    if ring:
        parts = results
    else:
        totals = []
        for value in results:
            value = value.astype(jnp.bfloat16).reshape(blocks, quads, ROWS, value.shape[-1])
            value = value.swapaxes(0, 1).reshape(quads, blocks * ROWS, value.shape[-1])
            totals.append(
                jnp.einsum("qst,qsd->qtd", pick, value, preferred_element_type=jnp.float32)
            )
        loss = totals[1]
        total = totals[0].astype(jnp.bfloat16).reshape(pairs, 2, 2, 2 * tokens, width)
        parts = [total[pair, :, lane] for lane in range(2) for pair in range(pairs)]
    own_parts, other_parts = [], []
    for pair in range(pairs):
        own_parts.append(parts[pair].reshape(4, tokens, -1))
        swapped = lax.ppermute(parts[pairs + pair], "core", [(0, 1), (1, 0)])
        other_parts.append(swapped.reshape(4, tokens, -1))

    splits = 2 if turn % 4 == 0 else 1
    lots = min(steps * splits, chips - 1)
    cuts = [steps * splits * n // lots for n in range(lots + 1)]
    filled = []

    def fill(number, behind):
        shift = cuts[number]
        count = cuts[number + 1] - shift
        specs = [pl.BlockSpec((BLOCK, lane_slots), lambda s, d=shift: (0, (s + d) // splits))]
        specs += [
            pl.BlockSpec((turn * 2 * ROWS, width), lambda s, d=shift: ((s + d) // splits, 0))
        ] * pairs
        operands = [grad if behind is None else after(grad, behind), *placed]
        aliases = {}
        if filled:
            specs.append(pl.BlockSpec(memory_space=pl.ANY))
            aliases = {len(operands): 0}
            operands.append(filled[-1])
        out, mark = call(
            functools.partial(head_kernel, turn, splits, shift, pairs),
            f"head_grad_{number}",
            (count,),
            specs,
            [
                pl.BlockSpec((turn // splits * BLOCK, width), lambda s, d=shift: (s + d, 0)),
                pl.BlockSpec((8, LANES), lambda s: (0, 0)),
            ],
            [
                jax.ShapeDtypeStruct(head.shape, jnp.bfloat16),
                jax.ShapeDtypeStruct((8, LANES), jnp.float32),
            ],
            turn * flops // lots,
            (head.size + pairs * x_rows * width) * 2 // lots,
            28,
            aliases=aliases,
        )(*operands)
        filled.append(out)
        return mark

    if ring:
        index_of = {int(o) % chips: n for n, o in enumerate(offsets)}
        half = width // 2
        sums, mark = [], None
        for step in range(1, chips + 1):
            operands, specs = [], []
            ends = [index_of[-step % chips], index_of[step % chips]]
            places = [(ends[0], half, 0), (ends[1], half, 1), (ends[0], LANES, width // LANES)]
            for source in (own_parts, other_parts):
                for at, columns, where in places:
                    operands.append(source[at // 4])
                    specs.append(
                        pl.BlockSpec(
                            (1, tokens, columns), lambda s, a=at % 4, w=where: (a, 0, w)
                        )
                    )
            for way in range(len(sums)):
                moved = lax.ppermute(sums[way], CHIPS, circle.ways[way])
                operands.append(moved if mark is None else after(moved, mark))
                specs.append(pl.BlockSpec(moved.shape, lambda s: (0, 0)))
            last = step == chips
            out_types = [(width, jnp.bfloat16), (LANES, jnp.float32)]
            if not last:
                out_types = [(half + LANES, jnp.bfloat16), (half, jnp.bfloat16)]
            sums = call(
                functools.partial(add_kernel, last),
                f"ring_sum_{step}",
                (1,),
                specs,
                [pl.BlockSpec((tokens, columns), lambda s: (0, 0)) for columns, _ in out_types],
                [jax.ShapeDtypeStruct((tokens, columns), kind) for columns, kind in out_types],
                len(operands) * tokens * half,
                len(operands) * tokens * half * 2,
                16,
            )(*operands)
            mark = fill(step - 1, sums[1]) if step <= lots else None
        hidden_grad, loss = sums
        token_loss = loss[:, 0]
    else:
        inverse = jnp.sum(
            jnp.where(source_of[None, :] == jnp.arange(devices)[:, None], jnp.arange(devices)[None], 0),
            axis=1,
        )
        loss = loss[:, :, 0].reshape(devices, tokens)
        loss = loss.at[inverse].get(mode="promise_in_bounds")
        loss = lax.all_to_all(loss, ALL, split_axis=0, concat_axis=0, tiled=True)
        token_loss = jnp.sum(loss, axis=0)
        total = [
            (own.astype(jnp.float32) + other.astype(jnp.float32)).astype(jnp.bfloat16)
            for own, other in zip(own_parts, other_parts)
        ]
        total = jnp.concatenate(total, axis=0).reshape(chips * tokens, width)
        hidden_grad = lax.psum_scatter(total, CHIPS, tiled=True)
        for number in range(lots):
            fill(number, None)
    head_grad = filled[-1]

    return hidden_grad, head_grad, token_loss


def solution(mesh):
    groups, tok, voc = (mesh.shape[name] for name in ("groups", "tok", "voc"))
    cores = Mesh(mesh.devices.reshape(groups, tok // 2, 2, voc), ("groups", "x", "core", "voc"))
    tokens_on = ("groups",) + ALL
    return jax.shard_map(
        on_device,
        mesh=cores,
        in_specs=(
            P(tokens_on, None),
            P(ALL, None),
            P(tokens_on, None),
            P(tokens_on),
            P(tokens_on, None, None),
        ),
        out_specs=(P(tokens_on, None), P(tokens_on, None), P(tokens_on)),
        check_vma=False,
    )
```

```python
import functools

import jax
import jax.numpy as jnp
import numpy as np
from jax import lax
from jax.experimental import pallas as pl
from jax.experimental.pallas import tpu as pltpu
from jax.sharding import Mesh
from jax.sharding import PartitionSpec as P

BLOCK = 128
LANES = 128
C = 2
QUAD = 4
ROWS = QUAD * C
COLS = 256
ALL = ("x", "core", "voc")
CHIPS = ("x", "voc")
RING_MOST = 8
MIB = 1024 * 1024
NT = (((1,), (1,)), ((), ()))


def call(kernel, name, grid, ins, outs, shapes, flops, moved, vmem, scratch=(), aliases=None):
    return pl.pallas_call(
        kernel,
        grid=grid,
        in_specs=ins,
        out_specs=outs,
        out_shape=shapes,
        scratch_shapes=scratch,
        input_output_aliases=aliases or {},
        compiler_params=pltpu.CompilerParams(
            dimension_semantics=("arbitrary",) * len(grid), vmem_limit_bytes=vmem * MIB
        ),
        cost_estimate=pl.CostEstimate(flops=flops, bytes_accessed=moved, transcendentals=0),
        name=name,
    )


def place_kernel(pick_ref, *refs):
    *held, out_ref = refs
    width = out_ref.shape[1]
    blocks = out_ref.shape[0] // (2 * ROWS)
    for start in range(0, width, COLS):
        quads = []
        for quad in range(2):
            values = [
                ref[:, start : start + COLS] for ref in held[quad * QUAD : (quad + 1) * QUAD]
            ]
            rows = jnp.dot(
                pick_ref[quad], jnp.concatenate(values, axis=0), preferred_element_type=jnp.float32
            )
            quads.append(rows.reshape(blocks, ROWS, COLS))
        both = jnp.concatenate(quads, axis=1).reshape(blocks * 2 * ROWS, COLS)
        out_ref[:, start : start + COLS] = both.astype(jnp.bfloat16)


def in_block(shape, axis, pairs, joint):
    slot = lax.broadcasted_iota(jnp.int32, shape, axis)
    group = pairs * joint * 2 * ROWS
    return slot // group * joint + slot % (joint * 2 * ROWS) // (2 * ROWS)


def joint_rows(x_refs, first, joint, columns=slice(None)):
    rows = slice(first * 2 * ROWS, (first + joint) * 2 * ROWS)
    return [ref[rows, columns] for ref in x_refs]


def sum_quad(spread, rows_ref, quad, columns):
    blocks = rows_ref.shape[0]
    rows = rows_ref[:, quad * ROWS : (quad + 1) * ROWS, columns]
    rows = rows.reshape(blocks * ROWS, rows.shape[-1]).astype(jnp.bfloat16)
    return jnp.dot(spread, rows, preferred_element_type=jnp.float32)


def two_parts(values):
    high = values.astype(jnp.bfloat16)
    low = (values - high.astype(jnp.float32)).astype(jnp.bfloat16)
    lane = lax.broadcasted_iota(jnp.int32, values.shape, 1)
    return jnp.where(lane < LANES // 2, high.astype(jnp.float32), low.astype(jnp.float32)).astype(
        jnp.bfloat16
    )


def joined(values):
    values = values.astype(jnp.float32)
    return values + pltpu.roll(values, LANES // 2, 1)


def main_kernel(turn, steps, pairs, sums, scale_ref, head_ref, teacher_ref, map_ref, *refs):
    x_refs = refs[:pairs]
    grad_ref, *loss_ref = refs[pairs:-2]
    rows_ref, slot_loss_ref = refs[-2:]
    step = pl.program_id(0)
    origin = step * turn if sums else 0
    scale = scale_ref[0]
    joint = 2 if turn % 2 == 0 else 1
    group = pairs * joint * 2 * ROWS
    own_block = in_block((group, BLOCK), 0, pairs, joint)
    logits = []
    for first in range(0, turn, joint):
        product = lax.dot_general(
            jnp.concatenate(joint_rows(x_refs, first, joint), axis=0),
            head_ref[first * BLOCK : (first + joint) * BLOCK, :],
            NT,
            preferred_element_type=jnp.float32,
        )
        part = product[:, :BLOCK]
        for k in range(1, joint):
            part = jnp.where(own_block == k, product[:, k * BLOCK : (k + 1) * BLOCK], part)
        logits.append(part)
    logits = jnp.concatenate(logits, axis=0)

    def log_softmax(values):
        top = jnp.max(values, axis=-1, keepdims=True)
        return values - top - jnp.log(jnp.sum(jnp.exp(values - top), axis=-1, keepdims=True))

    student_log = log_softmax(logits)
    teacher_log = log_softmax(teacher_ref[...].astype(jnp.float32))
    teacher_prob = jnp.exp(teacher_log)
    loss = scale * jnp.sum(teacher_prob * (teacher_log - student_log), axis=-1, keepdims=True)
    loss = jnp.broadcast_to(loss, logits.shape)
    grad = BLOCK * scale * (jnp.exp(student_log) - teacher_prob)
    grad_ref[...] = grad.T.astype(jnp.bfloat16)
    grad = grad.astype(jnp.bfloat16)

    for first in range(0, turn, joint):
        here = slice(first * pairs * 2 * ROWS, (first + joint) * pairs * 2 * ROWS)
        lines = [
            jnp.where(own_block == k, grad[here], jnp.zeros_like(grad[here])) for k in range(joint)
        ]
        grads = jnp.dot(
            jnp.concatenate(lines, axis=1),
            head_ref[first * BLOCK : (first + joint) * BLOCK, :],
            preferred_element_type=jnp.float32,
        )
        for pair in range(pairs):
            to = slice(pair * 2 * ROWS, (pair + 1) * 2 * ROWS)
            for k in range(joint):
                start = (pair * joint + k) * 2 * ROWS
                rows_ref[origin + first + k, to, :] = grads[start : start + 2 * ROWS].astype(
                    rows_ref.dtype
                )
                start += here.start
                slot_loss_ref[origin + first + k, to, :] = loss[start : start + 2 * ROWS]

    if not sums:
        return
    part_refs = loss_ref

    @pl.when(step == steps - 1)
    def _():
        half = part_refs[0].shape[0]
        width = rows_ref.shape[-1]
        for quad in range(2 * pairs):
            slots = map_ref[quad : quad + 1, :]
            token = lax.broadcasted_iota(jnp.int32, (2 * half, slots.shape[1]), 0)
            spread = jnp.where(slots == token, 1.0, 0.0).astype(jnp.bfloat16)

            def put(columns, total):
                part_refs[quad][:, columns] = total[:half]
                part_refs[2 * pairs + quad][:, columns] = total[half:]

            loss = sum_quad(spread, slot_loss_ref, quad, slice(0, LANES))
            put(slice(width, width + LANES), two_parts(loss))
            for start in range(0, width, COLS):
                columns = slice(start, start + COLS)
                put(columns, sum_quad(spread, rows_ref, quad, columns).astype(jnp.bfloat16))


def head_kernel(turn, splits, shift, pairs, grad_ref, *refs):
    x_refs, (out_ref, mark_ref) = refs[:pairs], refs[-2:]
    joint = 2 if turn % 2 == 0 else 1
    slots = grad_ref.shape[1]
    share = turn // splits
    place = in_block((1, slots), 1, pairs, joint) - (pl.program_id(0) + shift) % splits * share
    grad = grad_ref[...]
    spaced = [grad * (place == index).astype(jnp.bfloat16) for index in range(share)]
    spaced = jnp.concatenate(spaced, axis=0)
    for start in range(0, out_ref.shape[1], COLS):
        columns = slice(start, start + COLS)
        rows = [
            piece
            for first in range(0, turn, joint)
            for piece in joint_rows(x_refs, first, joint, columns)
        ]
        out_ref[:, columns] = jnp.dot(
            spaced, jnp.concatenate(rows, axis=0), preferred_element_type=jnp.float32
        ).astype(jnp.bfloat16)
    mark_ref[...] = jnp.zeros_like(mark_ref)


def add_kernel(last, *refs):
    own_right, own_left, own_loss, other_right, other_left, other_loss = refs[:6]
    half = own_right.shape[-1]
    moved, outs = (refs[6:], ()) if len(refs) == 8 else (refs[6:8], refs[8:])
    moved, outs = (moved, outs) if outs else ((), moved)

    def whole(ref):
        return ref[...].reshape(ref.shape[-2:]).astype(jnp.float32)

    right = whole(own_right) + whole(other_right)
    left = whole(own_left) + whole(other_left)
    loss = joined(whole(own_loss)) + joined(whole(other_loss))
    if moved:
        right += moved[0][:, :half].astype(jnp.float32)
        left += moved[1][...].astype(jnp.float32)
        loss += joined(moved[0][:, half:])
    if last:
        outs[0][:, :half] = right.astype(jnp.bfloat16)
        outs[0][:, half:] = left.astype(jnp.bfloat16)
        outs[1][...] = loss
    else:
        outs[0][:, :half] = right.astype(jnp.bfloat16)
        outs[0][:, half:] = two_parts(loss)
        outs[1][...] = left.astype(jnp.bfloat16)


def ring_order(rows, columns):
    order = []
    for r in range(rows):
        line = [r * columns + c for c in range(columns)]
        order += line if r % 2 == 0 else line[::-1]
    return order


def arrivals(chips):
    near = [-1, 1, 0]
    for step in range(2, chips // 2):
        near += [-step, step]
    return near + [chips // 2]


def after(value, *others):
    return lax.optimization_barrier((value, *others))[0]


class Ring:
    def __init__(self, hidden, order):
        chips = len(order)
        self.order = order
        self.ways = [
            [(order[p], order[(p + way) % chips]) for p in range(chips)] for way in (1, -1)
        ]
        self.moving = [hidden, hidden]
        self.got = {0: self.both(hidden)}

    def both(self, shard):
        return shard, lax.ppermute(shard, "core", [(0, 1), (1, 0)])

    def step(self, number, *behind):
        if behind:
            self.moving = [after(shard, *behind) for shard in self.moving]
        self.moving = [lax.ppermute(shard, CHIPS, way) for shard, way in zip(self.moving, self.ways)]
        self.got[-number], self.got[number] = (self.both(shard) for shard in self.moving)

    def last(self, *behind):
        shard = jnp.where(lax.axis_index("core") == 0, *self.moving)
        down = lax.axis_size("voc")

        def place(chip, core):
            return (chip // down * 2 + core) * down + chip % down

        links = [
            (place(source, core), place(target, core))
            for core in range(2)
            for source, target in self.ways[core]
        ]
        self.got[len(self.order) // 2] = self.both(lax.ppermute(after(shard, *behind), ALL, links))


def gather_whole(hidden):
    chips = lax.axis_size(CHIPS)
    own = lax.all_gather(hidden, CHIPS, axis=0)
    other = lax.ppermute(own, "core", [(0, 1), (1, 0)])
    return [(own[chip], other[chip]) for chip in range(chips)]


def on_device(hidden, head, block_ids, live_counts, teacher):
    across, down = lax.axis_size("x"), lax.axis_size("voc")
    chips = across * down
    devices = 2 * chips
    pairs = chips // 4
    tokens, list_width = block_ids.shape
    width = hidden.shape[1]
    blocks = head.shape[0] // BLOCK
    even = [n for n in range(2, 9, 2) if blocks % n == 0]
    turn = max(even) if even else 1
    steps = blocks // turn
    entries = tokens * list_width
    bucket = blocks * C
    per_block = devices * C
    core = lax.axis_index("core")
    ring = chips <= RING_MOST
    order = ring_order(across, down)
    if ring:
        circle = Ring(hidden, order)
        circle.step(1)
        offsets = np.array(arrivals(chips))
        places = np.argsort(np.array(order))
        spot = jnp.asarray(places, jnp.int32)[lax.axis_index(CHIPS)]
        chip_of = jnp.asarray(np.array(order), jnp.int32)[(spot + offsets) % chips]
    else:
        held = gather_whole(hidden)
        offsets = np.arange(chips)
        chip_of = jnp.arange(chips, dtype=jnp.int32)

    flat_ids = block_ids.reshape(entries)
    position = jnp.arange(entries, dtype=jnp.int32)
    earlier = (flat_ids[:, None] == flat_ids[None, :]) & (position[:, None] > position[None, :])
    ranks = jnp.sum(earlier, axis=1, dtype=jnp.int32)
    live = (jnp.arange(list_width, dtype=jnp.int32)[None, :] < live_counts[:, None]).reshape(entries)
    map_rows = -(-bucket // BLOCK)
    meta_at = -(-bucket // 16) * 16
    live_rows = tokens // BLOCK
    deep = meta_at + -(-(map_rows + live_rows) // 16) * 16
    rows = flat_ids // blocks * deep + ranks * blocks + flat_ids % blocks
    slots = jnp.arange(devices * deep, dtype=jnp.int32)
    place = (slots[:, None] == rows[None, :]).astype(jnp.bfloat16)
    send_teacher = jnp.dot(
        place, teacher.reshape(entries, BLOCK), preferred_element_type=jnp.float32
    ).astype(jnp.bfloat16)
    named = jnp.where(live, position // list_width + 1, 0)
    tight = flat_ids // blocks * bucket + ranks * blocks + flat_ids % blocks
    spots = jnp.arange(devices * bucket, dtype=jnp.int32)
    send_map = jnp.sum(jnp.where(tight[:, None] == spots[None, :], named[:, None], 0), axis=0)
    send_map = send_map.reshape(devices, bucket)
    send_map = jnp.pad(send_map, ((0, 0), (0, map_rows * BLOCK - bucket)))
    send_meta = jnp.concatenate(
        [
            send_map.reshape(devices, map_rows, BLOCK),
            jnp.broadcast_to(live_counts.reshape(1, live_rows, BLOCK), (devices, live_rows, BLOCK)),
            jnp.zeros((devices, deep - meta_at - map_rows - live_rows, BLOCK), jnp.int32),
        ],
        axis=1,
    ).astype(jnp.bfloat16)
    sent = lax.dynamic_update_slice(
        send_teacher.reshape(devices, deep, BLOCK), send_meta, (0, meta_at, 0)
    )
    if ring:
        sent = after(sent, *circle.moving)
        for number in range(2, chips // 2 - 1):
            circle.step(number)
    got = lax.all_to_all(sent, ALL, split_axis=0, concat_axis=0, tiled=True)

    lanes = jnp.stack([core, 1 - core])
    pair_of = chip_of.reshape(chips // 2, 1, 2)
    source_of = (pair_of // down * 2 + lanes[None, :, None]) * down + pair_of % down
    source_of = source_of.reshape(devices)
    got = got.at[source_of].get(mode="promise_in_bounds")
    meta = got[:, meta_at:].astype(jnp.int32)
    live_total = jnp.sum(meta[:, map_rows : map_rows + live_rows])
    scale = jnp.float32(tokens * devices) / live_total.astype(jnp.float32)
    slot_map = meta[:, :map_rows].reshape(devices, map_rows * BLOCK)[:, :bucket]
    quads = devices // QUAD
    slot_map = slot_map.reshape(quads, ROWS, blocks)
    offset = jnp.arange(ROWS, dtype=jnp.int32)[None, :, None] // C * tokens - 1
    slot_map = jnp.where(slot_map > 0, slot_map + offset, -1)
    slot_map = slot_map.swapaxes(1, 2).reshape(quads, blocks * ROWS)
    token_of = jnp.arange(QUAD * tokens, dtype=jnp.int32)
    pick = (slot_map[:, :, None] == token_of[None, None, :]).astype(jnp.bfloat16)
    if ring:
        circle.step(chips // 2 - 1, pick)
        held = [circle.got[int(offset)] for offset in offsets[:-1]]
    got_teacher = got[:, :bucket].reshape(devices, C, blocks, BLOCK)
    joint = 2 if turn % 2 == 0 else 1
    got_teacher = got_teacher.reshape(pairs, 2 * ROWS, blocks // joint, joint, BLOCK)
    got_teacher = got_teacher.transpose(2, 0, 3, 1, 4).reshape(blocks * per_block, BLOCK)

    once = pl.Buffered(1)
    x_rows = blocks * 2 * ROWS
    part = max(n for n in range(1, 17) if blocks % n == 0 and (n * ROWS) % 16 == 0)
    placed = []
    for pair in range(pairs):
        if ring and pair == pairs - 1:
            circle.last(*placed)
            held += [circle.got[int(offset)] for offset in offsets[len(held) :]]
        operands = []
        for quad in range(2):
            two = held[pair * 4 + quad * 2 : pair * 4 + quad * 2 + 2]
            operands += [chip[lane] for lane in range(2) for chip in two]
        placed.append(
            call(
                place_kernel,
                f"place_{pair}",
                (blocks // part,),
                [pl.BlockSpec((2, part * ROWS, QUAD * tokens), lambda s, p=pair: (p, s, 0))]
                + [pl.BlockSpec(o.shape, lambda s: (0, 0), pipeline_mode=once) for o in operands],
                pl.BlockSpec((part * 2 * ROWS, width), lambda s: (s, 0)),
                jax.ShapeDtypeStruct((x_rows, width), jnp.bfloat16),
                2 * x_rows * QUAD * tokens * width,
                2 * x_rows * width * 2,
                52,
            )(pick, *operands)
        )

    lane_slots = turn * per_block
    slot_spec = pl.BlockSpec((lane_slots, BLOCK), lambda s: (s, 0))
    flat_spec = pl.BlockSpec((BLOCK, lane_slots), lambda s: (0, s))
    x_spec = pl.BlockSpec((turn * 2 * ROWS, width), lambda s: (s, 0))
    flops = 2 * blocks * per_block * BLOCK * width
    if ring:
        part = (2 * tokens, width + LANES)
        out_specs = [pl.BlockSpec(part, lambda s: (0, 0), pipeline_mode=once)] * (2 * quads)
        out_shapes = [jax.ShapeDtypeStruct(part, jnp.bfloat16)] * (2 * quads)
        scratch = [
            pltpu.VMEM((blocks, per_block, width), jnp.float32),
            pltpu.VMEM((blocks, per_block, BLOCK), jnp.float32),
        ]
    else:
        out_specs = [
            pl.BlockSpec((turn, per_block, columns), lambda s: (s, 0, 0))
            for columns in (width, BLOCK)
        ]
        out_shapes = [
            jax.ShapeDtypeStruct((blocks, per_block, width), jnp.bfloat16),
            jax.ShapeDtypeStruct((blocks, per_block, BLOCK), jnp.float32),
        ]
        scratch = []
    grad, *results = call(
        functools.partial(main_kernel, turn, steps, pairs, ring),
        "logits_and_back",
        (steps,),
        [
            pl.BlockSpec(memory_space=pltpu.SMEM),
            pl.BlockSpec((turn * BLOCK, width), lambda s: (s, 0)),
            slot_spec,
            pl.BlockSpec(slot_map.shape, lambda s: (0, 0), pipeline_mode=once),
        ]
        + [x_spec] * pairs,
        [flat_spec] + out_specs,
        [jax.ShapeDtypeStruct((BLOCK, blocks * per_block), jnp.bfloat16)] + out_shapes,
        16 * flops,
        head.size * 2 + pairs * x_rows * width * 2,
        52,
        scratch,
    )(
        scale.reshape(1),
        head,
        got_teacher,
        slot_map,
        *placed,
    )
    if ring:
        parts = results
    else:
        totals = []
        for value in results:
            value = value.astype(jnp.bfloat16).reshape(blocks, quads, ROWS, value.shape[-1])
            value = value.swapaxes(0, 1).reshape(quads, blocks * ROWS, value.shape[-1])
            totals.append(
                jnp.einsum("qst,qsd->qtd", pick, value, preferred_element_type=jnp.float32)
            )
        loss = totals[1]
        total = totals[0].astype(jnp.bfloat16).reshape(quads, 2, 2 * tokens, width)
        parts = [total[quad, lane] for lane in range(2) for quad in range(quads)]
    own_parts, other_parts = [], []
    for quad in range(quads):
        own_parts.append(parts[quad].reshape(2, tokens, -1))
        swapped = lax.ppermute(parts[quads + quad], "core", [(0, 1), (1, 0)])
        other_parts.append(swapped.reshape(2, tokens, -1))

    splits = 2 if turn % 4 == 0 else 1
    lots = min(steps * splits, chips - 1)
    cuts = [steps * splits * n // lots for n in range(lots + 1)]
    filled = []

    def fill(number, behind):
        shift = cuts[number]
        count = cuts[number + 1] - shift
        specs = [pl.BlockSpec((BLOCK, lane_slots), lambda s, d=shift: (0, (s + d) // splits))]
        specs += [
            pl.BlockSpec((turn * 2 * ROWS, width), lambda s, d=shift: ((s + d) // splits, 0))
        ] * pairs
        operands = [grad if behind is None else after(grad, behind), *placed]
        aliases = {}
        if filled:
            specs.append(pl.BlockSpec(memory_space=pl.ANY))
            aliases = {len(operands): 0}
            operands.append(filled[-1])
        out, mark = call(
            functools.partial(head_kernel, turn, splits, shift, pairs),
            f"head_grad_{number}",
            (count,),
            specs,
            [
                pl.BlockSpec((turn // splits * BLOCK, width), lambda s, d=shift: (s + d, 0)),
                pl.BlockSpec((8, LANES), lambda s: (0, 0)),
            ],
            [
                jax.ShapeDtypeStruct(head.shape, jnp.bfloat16),
                jax.ShapeDtypeStruct((8, LANES), jnp.float32),
            ],
            turn * flops // lots,
            (head.size + pairs * x_rows * width) * 2 // lots,
            28,
            aliases=aliases,
        )(*operands)
        filled.append(out)
        return mark

    if ring:
        index_of = {int(o) % chips: n for n, o in enumerate(offsets)}
        half = width // 2
        sums, mark = [], None
        for step in range(1, chips + 1):
            operands, specs = [], []
            ends = [index_of[-step % chips], index_of[step % chips]]
            places = [(ends[0], half, 0), (ends[1], half, 1), (ends[0], LANES, width // LANES)]
            for source in (own_parts, other_parts):
                for at, columns, where in places:
                    operands.append(source[at // 2])
                    specs.append(
                        pl.BlockSpec(
                            (1, tokens, columns), lambda s, a=at % 2, w=where: (a, 0, w)
                        )
                    )
            for way in range(len(sums)):
                moved = lax.ppermute(sums[way], CHIPS, circle.ways[way])
                operands.append(moved if mark is None else after(moved, mark))
                specs.append(pl.BlockSpec(moved.shape, lambda s: (0, 0)))
            last = step == chips
            out_types = [(width, jnp.bfloat16), (LANES, jnp.float32)]
            if not last:
                out_types = [(half + LANES, jnp.bfloat16), (half, jnp.bfloat16)]
            sums = call(
                functools.partial(add_kernel, last),
                f"ring_sum_{step}",
                (1,),
                specs,
                [pl.BlockSpec((tokens, columns), lambda s: (0, 0)) for columns, _ in out_types],
                [jax.ShapeDtypeStruct((tokens, columns), kind) for columns, kind in out_types],
                len(operands) * tokens * half,
                len(operands) * tokens * half * 2,
                16,
            )(*operands)
            mark = fill(step - 1, sums[1]) if step <= lots else None
        hidden_grad, loss = sums
        token_loss = loss[:, 0]
    else:
        inverse = jnp.sum(
            jnp.where(source_of[None, :] == jnp.arange(devices)[:, None], jnp.arange(devices)[None], 0),
            axis=1,
        )
        loss = loss[:, :, 0].reshape(devices, tokens)
        loss = loss.at[inverse].get(mode="promise_in_bounds")
        loss = lax.all_to_all(loss, ALL, split_axis=0, concat_axis=0, tiled=True)
        token_loss = jnp.sum(loss, axis=0)
        total = [
            (own.astype(jnp.float32) + other.astype(jnp.float32)).astype(jnp.bfloat16)
            for own, other in zip(own_parts, other_parts)
        ]
        total = jnp.concatenate(total, axis=0).reshape(chips * tokens, width)
        hidden_grad = lax.psum_scatter(total, CHIPS, tiled=True)
        for number in range(lots):
            fill(number, None)
    head_grad = filled[-1]

    return hidden_grad, head_grad, token_loss


def solution(mesh):
    groups, tok, voc = (mesh.shape[name] for name in ("groups", "tok", "voc"))
    cores = Mesh(mesh.devices.reshape(groups, tok // 2, 2, voc), ("groups", "x", "core", "voc"))
    tokens_on = ("groups",) + ALL
    return jax.shard_map(
        on_device,
        mesh=cores,
        in_specs=(
            P(tokens_on, None),
            P(ALL, None),
            P(tokens_on, None),
            P(tokens_on),
            P(tokens_on, None, None),
        ),
        out_specs=(P(tokens_on, None), P(tokens_on, None), P(tokens_on)),
        check_vma=False,
    )
```

```python
import functools

import jax
import jax.numpy as jnp
import numpy as np
from jax import lax
from jax.experimental import pallas as pl
from jax.experimental.pallas import tpu as pltpu
from jax.sharding import Mesh
from jax.sharding import PartitionSpec as P

BLOCK = 128
LANES = 128
C = 2
QUAD = 4
ROWS = QUAD * C
COLS = 256
ALL = ("x", "core", "voc")
CHIPS = ("x", "voc")
RING_MOST = 8
MIB = 1024 * 1024
NT = (((1,), (1,)), ((), ()))


def call(kernel, name, grid, ins, outs, shapes, flops, moved, vmem, scratch=(), aliases=None):
    return pl.pallas_call(
        kernel,
        grid=grid,
        in_specs=ins,
        out_specs=outs,
        out_shape=shapes,
        scratch_shapes=scratch,
        input_output_aliases=aliases or {},
        compiler_params=pltpu.CompilerParams(
            dimension_semantics=("arbitrary",) * len(grid), vmem_limit_bytes=vmem * MIB
        ),
        cost_estimate=pl.CostEstimate(flops=flops, bytes_accessed=moved, transcendentals=0),
        name=name,
    )


def place_kernel(pick_ref, *refs):
    *held, out_ref = refs
    for start in range(0, out_ref.shape[1], COLS):
        columns = slice(start, start + COLS)
        values = jnp.concatenate([ref[:, columns] for ref in held], axis=0)
        rows = jnp.dot(pick_ref[0], values, preferred_element_type=jnp.float32)
        out_ref[:, columns] = rows.astype(jnp.bfloat16)


def in_block(shape, axis, quads, joint):
    slot = lax.broadcasted_iota(jnp.int32, shape, axis)
    return slot // (quads * joint * ROWS) * joint + slot % (joint * ROWS) // ROWS


def joint_rows(x_refs, first, joint, columns=slice(None)):
    rows = slice(first * ROWS, (first + joint) * ROWS)
    return [ref[rows, columns] for ref in x_refs]


def sum_quad(spread, rows_ref, quad, columns):
    blocks = rows_ref.shape[0]
    rows = rows_ref[:, quad * ROWS : (quad + 1) * ROWS, columns]
    rows = rows.reshape(blocks * ROWS, rows.shape[-1]).astype(jnp.bfloat16)
    return jnp.dot(spread, rows, preferred_element_type=jnp.float32)


def two_parts(values):
    high = values.astype(jnp.bfloat16)
    low = (values - high.astype(jnp.float32)).astype(jnp.bfloat16)
    lane = lax.broadcasted_iota(jnp.int32, values.shape, 1)
    return jnp.where(lane < LANES // 2, high.astype(jnp.float32), low.astype(jnp.float32)).astype(
        jnp.bfloat16
    )


def joined(values):
    values = values.astype(jnp.float32)
    return values + pltpu.roll(values, LANES // 2, 1)


def main_kernel(turn, steps, quads, sums, scale_ref, head_ref, teacher_ref, map_ref, *refs):
    x_refs = refs[:quads]
    grad_ref, *loss_ref = refs[quads:-2]
    rows_ref, slot_loss_ref = refs[-2:]
    step = pl.program_id(0)
    origin = step * turn if sums else 0
    scale = scale_ref[0]
    joint = 2 if turn % 2 == 0 else 1
    group = quads * joint * ROWS
    own_block = in_block((group, BLOCK), 0, quads, joint)
    logits = []
    for first in range(0, turn, joint):
        product = lax.dot_general(
            jnp.concatenate(joint_rows(x_refs, first, joint), axis=0),
            head_ref[first * BLOCK : (first + joint) * BLOCK, :],
            NT,
            preferred_element_type=jnp.float32,
        )
        part = product[:, :BLOCK]
        for k in range(1, joint):
            part = jnp.where(own_block == k, product[:, k * BLOCK : (k + 1) * BLOCK], part)
        logits.append(part)
    logits = jnp.concatenate(logits, axis=0)

    def log_softmax(values):
        top = jnp.max(values, axis=-1, keepdims=True)
        return values - top - jnp.log(jnp.sum(jnp.exp(values - top), axis=-1, keepdims=True))

    student_log = log_softmax(logits)
    teacher_log = log_softmax(teacher_ref[...].astype(jnp.float32))
    teacher_prob = jnp.exp(teacher_log)
    loss = scale * jnp.sum(teacher_prob * (teacher_log - student_log), axis=-1, keepdims=True)
    loss = jnp.broadcast_to(loss, logits.shape)
    grad = BLOCK * scale * (jnp.exp(student_log) - teacher_prob)
    grad_ref[...] = grad.T.astype(jnp.bfloat16)
    grad = grad.astype(jnp.bfloat16)

    for first in range(0, turn, joint):
        here = slice(first * quads * ROWS, (first + joint) * quads * ROWS)
        lines = [
            jnp.where(own_block == k, grad[here], jnp.zeros_like(grad[here])) for k in range(joint)
        ]
        grads = jnp.dot(
            jnp.concatenate(lines, axis=1),
            head_ref[first * BLOCK : (first + joint) * BLOCK, :],
            preferred_element_type=jnp.float32,
        )
        for quad in range(quads):
            to = slice(quad * ROWS, (quad + 1) * ROWS)
            for k in range(joint):
                start = (quad * joint + k) * ROWS
                rows_ref[origin + first + k, to, :] = grads[start : start + ROWS].astype(
                    rows_ref.dtype
                )
                start += here.start
                slot_loss_ref[origin + first + k, to, :] = loss[start : start + ROWS]

    if not sums:
        return
    part_refs = loss_ref

    @pl.when(step == steps - 1)
    def _():
        half = part_refs[0].shape[0]
        width = rows_ref.shape[-1]
        for quad in range(quads):
            slots = map_ref[quad : quad + 1, :]
            token = lax.broadcasted_iota(jnp.int32, (2 * half, slots.shape[1]), 0)
            spread = jnp.where(slots == token, 1.0, 0.0).astype(jnp.bfloat16)

            def put(columns, total):
                part_refs[quad][:, columns] = total[:half]
                part_refs[quads + quad][:, columns] = total[half:]

            loss = sum_quad(spread, slot_loss_ref, quad, slice(0, LANES))
            put(slice(width, width + LANES), two_parts(loss))
            for start in range(0, width, COLS):
                columns = slice(start, start + COLS)
                put(columns, sum_quad(spread, rows_ref, quad, columns).astype(jnp.bfloat16))


def head_kernel(turn, splits, shift, quads, grad_ref, *refs):
    x_refs, (out_ref, mark_ref) = refs[:quads], refs[-2:]
    joint = 2 if turn % 2 == 0 else 1
    slots = grad_ref.shape[1]
    share = turn // splits
    place = in_block((1, slots), 1, quads, joint) - (pl.program_id(0) + shift) % splits * share
    grad = grad_ref[...]
    spaced = [grad * (place == index).astype(jnp.bfloat16) for index in range(share)]
    spaced = jnp.concatenate(spaced, axis=0)
    for start in range(0, out_ref.shape[1], COLS):
        columns = slice(start, start + COLS)
        rows = [
            piece
            for first in range(0, turn, joint)
            for piece in joint_rows(x_refs, first, joint, columns)
        ]
        out_ref[:, columns] = jnp.dot(
            spaced, jnp.concatenate(rows, axis=0), preferred_element_type=jnp.float32
        ).astype(jnp.bfloat16)
    mark_ref[...] = jnp.zeros_like(mark_ref)


def add_kernel(last, *refs):
    own_right, own_left, own_loss, other_right, other_left, other_loss = refs[:6]
    half = own_right.shape[-1]
    moved, outs = (refs[6:], ()) if len(refs) == 8 else (refs[6:8], refs[8:])
    moved, outs = (moved, outs) if outs else ((), moved)

    def whole(ref):
        return ref[...].reshape(ref.shape[-2:]).astype(jnp.float32)

    right = whole(own_right) + whole(other_right)
    left = whole(own_left) + whole(other_left)
    loss = joined(whole(own_loss)) + joined(whole(other_loss))
    if moved:
        right += moved[0][:, :half].astype(jnp.float32)
        left += moved[1][...].astype(jnp.float32)
        loss += joined(moved[0][:, half:])
    if last:
        outs[0][:, :half] = right.astype(jnp.bfloat16)
        outs[0][:, half:] = left.astype(jnp.bfloat16)
        outs[1][...] = loss
    else:
        outs[0][:, :half] = right.astype(jnp.bfloat16)
        outs[0][:, half:] = two_parts(loss)
        outs[1][...] = left.astype(jnp.bfloat16)


def ring_order(rows, columns):
    order = []
    for r in range(rows):
        line = [r * columns + c for c in range(columns)]
        order += line if r % 2 == 0 else line[::-1]
    return order


def arrivals(chips):
    near = [-1, 1, 0]
    for step in range(2, chips // 2):
        near += [-step, step]
    return near + [chips // 2]


def after(value, *others):
    return lax.optimization_barrier((value, *others))[0]


class Ring:
    def __init__(self, hidden, order):
        chips = len(order)
        self.order = order
        self.ways = [
            [(order[p], order[(p + way) % chips]) for p in range(chips)] for way in (1, -1)
        ]
        self.moving = [hidden, hidden]
        self.got = {0: self.both(hidden)}

    def both(self, shard):
        return shard, lax.ppermute(shard, "core", [(0, 1), (1, 0)])

    def step(self, number, *behind):
        if behind:
            self.moving = [after(shard, *behind) for shard in self.moving]
        self.moving = [lax.ppermute(shard, CHIPS, way) for shard, way in zip(self.moving, self.ways)]
        self.got[-number], self.got[number] = (self.both(shard) for shard in self.moving)

    def last(self, before, beside):
        shard = jnp.where(lax.axis_index("core") == 0, *self.moving)
        down = lax.axis_size("voc")

        def place(chip, core):
            return (chip // down * 2 + core) * down + chip % down

        links = [
            (place(source, core), place(target, core))
            for core in range(2)
            for source, target in self.ways[core]
        ]
        shard = lax.ppermute(after(shard, *before), ALL, links)
        self.got[len(self.order) // 2] = self.both(after(shard, *beside))


def gather_whole(hidden):
    chips = lax.axis_size(CHIPS)
    own = lax.all_gather(hidden, CHIPS, axis=0)
    other = lax.ppermute(own, "core", [(0, 1), (1, 0)])
    return [(own[chip], other[chip]) for chip in range(chips)]


def on_device(hidden, head, block_ids, live_counts, teacher):
    across, down = lax.axis_size("x"), lax.axis_size("voc")
    chips = across * down
    devices = 2 * chips
    quads = devices // QUAD
    tokens, list_width = block_ids.shape
    width = hidden.shape[1]
    blocks = head.shape[0] // BLOCK
    even = [n for n in range(2, 9, 2) if blocks % n == 0]
    turn = max(even) if even else 1
    steps = blocks // turn
    entries = tokens * list_width
    bucket = blocks * C
    per_block = devices * C
    core = lax.axis_index("core")
    ring = chips <= RING_MOST
    order = ring_order(across, down)
    if ring:
        circle = Ring(hidden, order)
        circle.step(1)
        offsets = np.array(arrivals(chips))
        places = np.argsort(np.array(order))
        spot = jnp.asarray(places, jnp.int32)[lax.axis_index(CHIPS)]
        chip_of = jnp.asarray(np.array(order), jnp.int32)[(spot + offsets) % chips]
    else:
        held = gather_whole(hidden)
        offsets = np.arange(chips)
        chip_of = jnp.arange(chips, dtype=jnp.int32)

    flat_ids = block_ids.reshape(entries)
    position = jnp.arange(entries, dtype=jnp.int32)
    earlier = (flat_ids[:, None] == flat_ids[None, :]) & (position[:, None] > position[None, :])
    ranks = jnp.sum(earlier, axis=1, dtype=jnp.int32)
    live = (jnp.arange(list_width, dtype=jnp.int32)[None, :] < live_counts[:, None]).reshape(entries)
    map_rows = -(-bucket // BLOCK)
    meta_at = -(-bucket // 16) * 16
    live_rows = tokens // BLOCK
    deep = meta_at + -(-(map_rows + live_rows) // 16) * 16
    rows = flat_ids // blocks * deep + ranks * blocks + flat_ids % blocks
    slots = jnp.arange(devices * deep, dtype=jnp.int32)
    place = (slots[:, None] == rows[None, :]).astype(jnp.bfloat16)
    send_teacher = jnp.dot(
        place, teacher.reshape(entries, BLOCK), preferred_element_type=jnp.float32
    ).astype(jnp.bfloat16)
    named = jnp.where(live, position // list_width + 1, 0)
    tight = flat_ids // blocks * bucket + ranks * blocks + flat_ids % blocks
    spots = jnp.arange(devices * bucket, dtype=jnp.int32)
    send_map = jnp.sum(jnp.where(tight[:, None] == spots[None, :], named[:, None], 0), axis=0)
    send_map = send_map.reshape(devices, bucket)
    send_map = jnp.pad(send_map, ((0, 0), (0, map_rows * BLOCK - bucket)))
    send_meta = jnp.concatenate(
        [
            send_map.reshape(devices, map_rows, BLOCK),
            jnp.broadcast_to(live_counts.reshape(1, live_rows, BLOCK), (devices, live_rows, BLOCK)),
            jnp.zeros((devices, deep - meta_at - map_rows - live_rows, BLOCK), jnp.int32),
        ],
        axis=1,
    ).astype(jnp.bfloat16)
    sent = lax.dynamic_update_slice(
        send_teacher.reshape(devices, deep, BLOCK), send_meta, (0, meta_at, 0)
    )
    lanes = jnp.stack([core, 1 - core])
    pair_of = chip_of.reshape(chips // 2, 1, 2)
    source_of = (pair_of // down * 2 + lanes[None, :, None]) * down + pair_of % down
    source_of = source_of.reshape(devices)
    if ring:
        sent = after(sent, *circle.moving, source_of)
        for number in range(2, chips // 2 - 1):
            circle.step(number)
    got = lax.all_to_all(sent, ALL, split_axis=0, concat_axis=0, tiled=True)

    got = got.at[source_of].get(mode="promise_in_bounds")
    meta = got[:, meta_at:].astype(jnp.int32)
    live_total = jnp.sum(meta[:, map_rows : map_rows + live_rows])
    scale = jnp.float32(tokens * devices) / live_total.astype(jnp.float32)
    slot_map = meta[:, :map_rows].reshape(devices, map_rows * BLOCK)[:, :bucket]
    slot_map = slot_map.reshape(quads, ROWS, blocks)
    offset = jnp.arange(ROWS, dtype=jnp.int32)[None, :, None] // C * tokens - 1
    slot_map = jnp.where(slot_map > 0, slot_map + offset, -1)
    slot_map = slot_map.swapaxes(1, 2).reshape(quads, blocks * ROWS)
    token_of = jnp.arange(QUAD * tokens, dtype=jnp.int32)
    pick = (slot_map[:, :, None] == token_of[None, None, :]).astype(jnp.bfloat16)
    if ring:
        circle.step(chips // 2 - 1, pick)
        held = [circle.got[int(offset)] for offset in offsets[:-1]]
    got_teacher = got[:, :bucket].reshape(devices, C, blocks, BLOCK)
    joint = 2 if turn % 2 == 0 else 1
    got_teacher = got_teacher.reshape(quads, ROWS, blocks // joint, joint, BLOCK)
    got_teacher = got_teacher.transpose(2, 0, 3, 1, 4).reshape(blocks * per_block, BLOCK)

    once = pl.Buffered(1)
    x_rows = blocks * ROWS
    part = max(n for n in range(1, 17) if blocks % n == 0 and (n * ROWS) % 16 == 0)
    placed = []
    for quad in range(quads):
        if ring and quad == quads - 1:
            circle.last((*placed[:-1], got_teacher, scale), placed[-1:])
            held += [circle.got[int(offset)] for offset in offsets[len(held) :]]
        two = held[quad * 2 : quad * 2 + 2]
        operands = [chip[lane] for lane in range(2) for chip in two]
        placed.append(
            call(
                place_kernel,
                f"place_{quad}",
                (blocks // part,),
                [pl.BlockSpec((1, part * ROWS, QUAD * tokens), lambda s, q=quad: (q, s, 0))]
                + [pl.BlockSpec(o.shape, lambda s: (0, 0), pipeline_mode=once) for o in operands],
                pl.BlockSpec((part * ROWS, width), lambda s: (s, 0)),
                jax.ShapeDtypeStruct((x_rows, width), jnp.bfloat16),
                2 * x_rows * QUAD * tokens * width,
                2 * x_rows * width * 2,
                52,
            )(pick, *operands)
        )

    lane_slots = turn * per_block
    slot_spec = pl.BlockSpec((lane_slots, BLOCK), lambda s: (s, 0))
    flat_spec = pl.BlockSpec((BLOCK, lane_slots), lambda s: (0, s))
    x_spec = pl.BlockSpec((turn * ROWS, width), lambda s: (s, 0))
    flops = 2 * blocks * per_block * BLOCK * width
    if ring:
        part = (2 * tokens, width + LANES)
        out_specs = [pl.BlockSpec(part, lambda s: (0, 0), pipeline_mode=once)] * (2 * quads)
        out_shapes = [jax.ShapeDtypeStruct(part, jnp.bfloat16)] * (2 * quads)
        scratch = [
            pltpu.VMEM((blocks, per_block, width), jnp.float32),
            pltpu.VMEM((blocks, per_block, BLOCK), jnp.float32),
        ]
    else:
        out_specs = [
            pl.BlockSpec((turn, per_block, columns), lambda s: (s, 0, 0))
            for columns in (width, BLOCK)
        ]
        out_shapes = [
            jax.ShapeDtypeStruct((blocks, per_block, width), jnp.bfloat16),
            jax.ShapeDtypeStruct((blocks, per_block, BLOCK), jnp.float32),
        ]
        scratch = []
    grad, *results = call(
        functools.partial(main_kernel, turn, steps, quads, ring),
        "logits_and_back",
        (steps,),
        [
            pl.BlockSpec(memory_space=pltpu.SMEM),
            pl.BlockSpec((turn * BLOCK, width), lambda s: (s, 0)),
            slot_spec,
            pl.BlockSpec(slot_map.shape, lambda s: (0, 0), pipeline_mode=once),
        ]
        + [x_spec] * quads,
        [flat_spec] + out_specs,
        [jax.ShapeDtypeStruct((BLOCK, blocks * per_block), jnp.bfloat16)] + out_shapes,
        16 * flops,
        head.size * 2 + quads * x_rows * width * 2,
        52,
        scratch,
    )(
        scale.reshape(1),
        head,
        got_teacher,
        slot_map,
        *placed,
    )
    if ring:
        parts = results
    else:
        totals = []
        for value in results:
            value = value.astype(jnp.bfloat16).reshape(blocks, quads, ROWS, value.shape[-1])
            value = value.swapaxes(0, 1).reshape(quads, blocks * ROWS, value.shape[-1])
            totals.append(
                jnp.einsum("qst,qsd->qtd", pick, value, preferred_element_type=jnp.float32)
            )
        loss = totals[1]
        total = totals[0].astype(jnp.bfloat16).reshape(quads, 2, 2 * tokens, width)
        parts = [total[quad, lane] for lane in range(2) for quad in range(quads)]
    own_parts, other_parts = [], []
    for quad in range(quads):
        own_parts.append(parts[quad].reshape(2, tokens, -1))
        swapped = lax.ppermute(parts[quads + quad], "core", [(0, 1), (1, 0)])
        other_parts.append(swapped.reshape(2, tokens, -1))

    splits = 2 if turn % 4 == 0 else 1
    lots = min(steps * splits, chips - 1)
    cuts = [steps * splits * n // lots for n in range(lots + 1)]
    filled = []

    def fill(number, behind):
        shift = cuts[number]
        count = cuts[number + 1] - shift
        specs = [pl.BlockSpec((BLOCK, lane_slots), lambda s, d=shift: (0, (s + d) // splits))]
        specs += [
            pl.BlockSpec((turn * ROWS, width), lambda s, d=shift: ((s + d) // splits, 0))
        ] * quads
        operands = [grad if behind is None else after(grad, behind), *placed]
        aliases = {}
        if filled:
            specs.append(pl.BlockSpec(memory_space=pl.ANY))
            aliases = {len(operands): 0}
            operands.append(filled[-1])
        out, mark = call(
            functools.partial(head_kernel, turn, splits, shift, quads),
            f"head_grad_{number}",
            (count,),
            specs,
            [
                pl.BlockSpec((turn // splits * BLOCK, width), lambda s, d=shift: (s + d, 0)),
                pl.BlockSpec((8, LANES), lambda s: (0, 0)),
            ],
            [
                jax.ShapeDtypeStruct(head.shape, jnp.bfloat16),
                jax.ShapeDtypeStruct((8, LANES), jnp.float32),
            ],
            turn * flops // lots,
            (head.size + quads * x_rows * width) * 2 // lots,
            28,
            aliases=aliases,
        )(*operands)
        filled.append(out)
        return mark

    if ring:
        index_of = {int(o) % chips: n for n, o in enumerate(offsets)}
        half = width // 2
        sums, mark = [], None
        for step in range(1, chips + 1):
            operands, specs = [], []
            ends = [index_of[-step % chips], index_of[step % chips]]
            places = [(ends[0], half, 0), (ends[1], half, 1), (ends[0], LANES, width // LANES)]
            for source in (own_parts, other_parts):
                for at, columns, where in places:
                    operands.append(source[at // 2])
                    specs.append(
                        pl.BlockSpec(
                            (1, tokens, columns), lambda s, a=at % 2, w=where: (a, 0, w)
                        )
                    )
            for way in range(len(sums)):
                moved = lax.ppermute(sums[way], CHIPS, circle.ways[way])
                operands.append(moved if mark is None else after(moved, mark))
                specs.append(pl.BlockSpec(moved.shape, lambda s: (0, 0)))
            last = step == chips
            out_types = [(width, jnp.bfloat16), (LANES, jnp.float32)]
            if not last:
                out_types = [(half + LANES, jnp.bfloat16), (half, jnp.bfloat16)]
            sums = call(
                functools.partial(add_kernel, last),
                f"ring_sum_{step}",
                (1,),
                specs,
                [pl.BlockSpec((tokens, columns), lambda s: (0, 0)) for columns, _ in out_types],
                [jax.ShapeDtypeStruct((tokens, columns), kind) for columns, kind in out_types],
                len(operands) * tokens * half,
                len(operands) * tokens * half * 2,
                16,
            )(*operands)
            mark = fill(step - 1, sums[1]) if step <= lots else None
        hidden_grad, loss = sums
        token_loss = loss[:, 0]
    else:
        inverse = jnp.sum(
            jnp.where(source_of[None, :] == jnp.arange(devices)[:, None], jnp.arange(devices)[None], 0),
            axis=1,
        )
        loss = loss[:, :, 0].reshape(devices, tokens)
        loss = loss.at[inverse].get(mode="promise_in_bounds")
        loss = lax.all_to_all(loss, ALL, split_axis=0, concat_axis=0, tiled=True)
        token_loss = jnp.sum(loss, axis=0)
        total = [
            (own.astype(jnp.float32) + other.astype(jnp.float32)).astype(jnp.bfloat16)
            for own, other in zip(own_parts, other_parts)
        ]
        total = jnp.concatenate(total, axis=0).reshape(chips * tokens, width)
        hidden_grad = lax.psum_scatter(total, CHIPS, tiled=True)
        for number in range(lots):
            fill(number, None)
    head_grad = filled[-1]

    return hidden_grad, head_grad, token_loss


def solution(mesh):
    groups, tok, voc = (mesh.shape[name] for name in ("groups", "tok", "voc"))
    cores = Mesh(mesh.devices.reshape(groups, tok // 2, 2, voc), ("groups", "x", "core", "voc"))
    tokens_on = ("groups",) + ALL
    return jax.shard_map(
        on_device,
        mesh=cores,
        in_specs=(
            P(tokens_on, None),
            P(ALL, None),
            P(tokens_on, None),
            P(tokens_on),
            P(tokens_on, None, None),
        ),
        out_specs=(P(tokens_on, None), P(tokens_on, None), P(tokens_on)),
        check_vma=False,
    )
```

```python
import functools

import jax
import jax.numpy as jnp
import numpy as np
from jax import lax
from jax.experimental import pallas as pl
from jax.experimental.pallas import tpu as pltpu
from jax.sharding import Mesh
from jax.sharding import PartitionSpec as P

BLOCK = 128
LANES = 128
C = 2
QUAD = 4
ROWS = QUAD * C
COLS = 256
ALL = ("x", "core", "voc")
CHIPS = ("x", "voc")
RING_MOST = 8
MIB = 1024 * 1024
NT = (((1,), (1,)), ((), ()))


def call(kernel, name, grid, ins, outs, shapes, flops, moved, vmem, scratch=(), aliases=None):
    return pl.pallas_call(
        kernel,
        grid=grid,
        in_specs=ins,
        out_specs=outs,
        out_shape=shapes,
        scratch_shapes=scratch,
        input_output_aliases=aliases or {},
        compiler_params=pltpu.CompilerParams(
            dimension_semantics=("arbitrary",) * len(grid), vmem_limit_bytes=vmem * MIB
        ),
        cost_estimate=pl.CostEstimate(flops=flops, bytes_accessed=moved, transcendentals=0),
        name=name,
    )


def place_kernel(pick_ref, *refs):
    count = pick_ref.shape[0]
    held, outs = refs[: count * QUAD], refs[count * QUAD :]
    for start in range(0, outs[0].shape[1], COLS):
        columns = slice(start, start + COLS)
        for quad, out_ref in enumerate(outs):
            values = [ref[:, columns] for ref in held[quad * QUAD : (quad + 1) * QUAD]]
            rows = jnp.dot(
                pick_ref[quad], jnp.concatenate(values, axis=0), preferred_element_type=jnp.float32
            )
            out_ref[:, columns] = rows.astype(jnp.bfloat16)


def in_block(shape, axis, quads, joint):
    slot = lax.broadcasted_iota(jnp.int32, shape, axis)
    return slot // (quads * joint * ROWS) * joint + slot % (joint * ROWS) // ROWS


def joint_rows(x_refs, first, joint, columns=slice(None)):
    rows = slice(first * ROWS, (first + joint) * ROWS)
    return [ref[rows, columns] for ref in x_refs]


def sum_quad(spread, rows_ref, quad, columns):
    blocks = rows_ref.shape[0]
    rows = rows_ref[:, quad * ROWS : (quad + 1) * ROWS, columns]
    rows = rows.reshape(blocks * ROWS, rows.shape[-1]).astype(jnp.bfloat16)
    return jnp.dot(spread, rows, preferred_element_type=jnp.float32)


def two_parts(values):
    high = values.astype(jnp.bfloat16)
    low = (values - high.astype(jnp.float32)).astype(jnp.bfloat16)
    lane = lax.broadcasted_iota(jnp.int32, values.shape, 1)
    return jnp.where(lane < LANES // 2, high.astype(jnp.float32), low.astype(jnp.float32)).astype(
        jnp.bfloat16
    )


def joined(values):
    values = values.astype(jnp.float32)
    return values + pltpu.roll(values, LANES // 2, 1)


def main_kernel(turn, steps, quads, sums, scale_ref, head_ref, teacher_ref, map_ref, *refs):
    x_refs = refs[:quads]
    grad_ref, *loss_ref = refs[quads:-2]
    rows_ref, slot_loss_ref = refs[-2:]
    step = pl.program_id(0)
    origin = step * turn if sums else 0
    scale = scale_ref[0]
    joint = 2 if turn % 2 == 0 else 1
    group = quads * joint * ROWS
    own_block = in_block((group, BLOCK), 0, quads, joint)
    logits = []
    for first in range(0, turn, joint):
        product = lax.dot_general(
            jnp.concatenate(joint_rows(x_refs, first, joint), axis=0),
            head_ref[first * BLOCK : (first + joint) * BLOCK, :],
            NT,
            preferred_element_type=jnp.float32,
        )
        part = product[:, :BLOCK]
        for k in range(1, joint):
            part = jnp.where(own_block == k, product[:, k * BLOCK : (k + 1) * BLOCK], part)
        logits.append(part)
    logits = jnp.concatenate(logits, axis=0)

    def log_softmax(values):
        top = jnp.max(values, axis=-1, keepdims=True)
        return values - top - jnp.log(jnp.sum(jnp.exp(values - top), axis=-1, keepdims=True))

    student_log = log_softmax(logits)
    teacher_log = log_softmax(teacher_ref[...].astype(jnp.float32))
    teacher_prob = jnp.exp(teacher_log)
    loss = scale * jnp.sum(teacher_prob * (teacher_log - student_log), axis=-1, keepdims=True)
    loss = jnp.broadcast_to(loss, logits.shape)
    grad = BLOCK * scale * (jnp.exp(student_log) - teacher_prob)
    grad_ref[...] = grad.T.astype(jnp.bfloat16)
    grad = grad.astype(jnp.bfloat16)

    for first in range(0, turn, joint):
        here = slice(first * quads * ROWS, (first + joint) * quads * ROWS)
        lines = [
            jnp.where(own_block == k, grad[here], jnp.zeros_like(grad[here])) for k in range(joint)
        ]
        grads = jnp.dot(
            jnp.concatenate(lines, axis=1),
            head_ref[first * BLOCK : (first + joint) * BLOCK, :],
            preferred_element_type=jnp.float32,
        )
        for quad in range(quads):
            to = slice(quad * ROWS, (quad + 1) * ROWS)
            for k in range(joint):
                start = (quad * joint + k) * ROWS
                rows_ref[origin + first + k, to, :] = grads[start : start + ROWS].astype(
                    rows_ref.dtype
                )
                start += here.start
                slot_loss_ref[origin + first + k, to, :] = loss[start : start + ROWS]

    if not sums:
        return
    part_refs = loss_ref

    @pl.when(step == steps - 1)
    def _():
        half = part_refs[0].shape[0]
        width = rows_ref.shape[-1]
        for quad in range(quads):
            slots = map_ref[quad : quad + 1, :]
            token = lax.broadcasted_iota(jnp.int32, (2 * half, slots.shape[1]), 0)
            spread = jnp.where(slots == token, 1.0, 0.0).astype(jnp.bfloat16)

            def put(columns, total):
                part_refs[quad][:, columns] = total[:half]
                part_refs[quads + quad][:, columns] = total[half:]

            loss = sum_quad(spread, slot_loss_ref, quad, slice(0, LANES))
            put(slice(width, width + LANES), two_parts(loss))
            for start in range(0, width, COLS):
                columns = slice(start, start + COLS)
                put(columns, sum_quad(spread, rows_ref, quad, columns).astype(jnp.bfloat16))


def head_kernel(turn, splits, shift, quads, grad_ref, *refs):
    x_refs, (out_ref, mark_ref) = refs[:quads], refs[-2:]
    joint = 2 if turn % 2 == 0 else 1
    slots = grad_ref.shape[1]
    share = turn // splits
    place = in_block((1, slots), 1, quads, joint) - (pl.program_id(0) + shift) % splits * share
    grad = grad_ref[...]
    spaced = [grad * (place == index).astype(jnp.bfloat16) for index in range(share)]
    spaced = jnp.concatenate(spaced, axis=0)
    for start in range(0, out_ref.shape[1], COLS):
        columns = slice(start, start + COLS)
        rows = [
            piece
            for first in range(0, turn, joint)
            for piece in joint_rows(x_refs, first, joint, columns)
        ]
        out_ref[:, columns] = jnp.dot(
            spaced, jnp.concatenate(rows, axis=0), preferred_element_type=jnp.float32
        ).astype(jnp.bfloat16)
    mark_ref[...] = jnp.zeros_like(mark_ref)


def add_kernel(last, *refs):
    own_right, own_left, own_loss, other_right, other_left, other_loss = refs[:6]
    half = own_right.shape[-1]
    moved, outs = (refs[6:], ()) if len(refs) == 8 else (refs[6:8], refs[8:])
    moved, outs = (moved, outs) if outs else ((), moved)

    def whole(ref):
        return ref[...].reshape(ref.shape[-2:]).astype(jnp.float32)

    right = whole(own_right) + whole(other_right)
    left = whole(own_left) + whole(other_left)
    loss = joined(whole(own_loss)) + joined(whole(other_loss))
    if moved:
        right += moved[0][:, :half].astype(jnp.float32)
        left += moved[1][...].astype(jnp.float32)
        loss += joined(moved[0][:, half:])
    if last:
        outs[0][:, :half] = right.astype(jnp.bfloat16)
        outs[0][:, half:] = left.astype(jnp.bfloat16)
        outs[1][...] = loss
    else:
        outs[0][:, :half] = right.astype(jnp.bfloat16)
        outs[0][:, half:] = two_parts(loss)
        outs[1][...] = left.astype(jnp.bfloat16)


def ring_order(rows, columns):
    order = []
    for r in range(rows):
        line = [r * columns + c for c in range(columns)]
        order += line if r % 2 == 0 else line[::-1]
    return order


def arrivals(chips):
    near = [-1, 1, 0]
    for step in range(2, chips // 2):
        near += [-step, step]
    return near + [chips // 2]


def after(value, *others):
    return lax.optimization_barrier((value, *others))[0]


class Ring:
    def __init__(self, hidden, order):
        chips = len(order)
        self.order = order
        self.ways = [
            [(order[p], order[(p + way) % chips]) for p in range(chips)] for way in (1, -1)
        ]
        self.moving = [hidden, hidden]
        self.got = {0: self.both(hidden)}

    def both(self, shard):
        return shard, lax.ppermute(shard, "core", [(0, 1), (1, 0)])

    def step(self, number, *behind):
        if behind:
            self.moving = [after(shard, *behind) for shard in self.moving]
        self.moving = [lax.ppermute(shard, CHIPS, way) for shard, way in zip(self.moving, self.ways)]
        self.got[-number], self.got[number] = (self.both(shard) for shard in self.moving)

    def last(self, before, beside):
        shard = jnp.where(lax.axis_index("core") == 0, *self.moving)
        down = lax.axis_size("voc")

        def place(chip, core):
            return (chip // down * 2 + core) * down + chip % down

        links = [
            (place(source, core), place(target, core))
            for core in range(2)
            for source, target in self.ways[core]
        ]
        shard = lax.ppermute(after(shard, *before), ALL, links)
        self.got[len(self.order) // 2] = self.both(after(shard, *beside))


def gather_whole(hidden):
    chips = lax.axis_size(CHIPS)
    own = lax.all_gather(hidden, CHIPS, axis=0)
    other = lax.ppermute(own, "core", [(0, 1), (1, 0)])
    return [(own[chip], other[chip]) for chip in range(chips)]


def on_device(hidden, head, block_ids, live_counts, teacher):
    across, down = lax.axis_size("x"), lax.axis_size("voc")
    chips = across * down
    devices = 2 * chips
    quads = devices // QUAD
    tokens, list_width = block_ids.shape
    width = hidden.shape[1]
    blocks = head.shape[0] // BLOCK
    even = [n for n in range(2, 9, 2) if blocks % n == 0]
    turn = max(even) if even else 1
    steps = blocks // turn
    entries = tokens * list_width
    bucket = blocks * C
    per_block = devices * C
    core = lax.axis_index("core")
    ring = chips <= RING_MOST
    order = ring_order(across, down)
    if ring:
        circle = Ring(hidden, order)
        circle.step(1)
        offsets = np.array(arrivals(chips))

        def turned(place):
            line, spot = place // down, place % down
            return line * down + jnp.where(line % 2 == 0, spot, down - 1 - spot)

        chip_of = turned((turned(lax.axis_index(CHIPS)) + offsets + chips) % chips)
    else:
        held = gather_whole(hidden)
        offsets = np.arange(chips)
        chip_of = jnp.arange(chips, dtype=jnp.int32)

    flat_ids = block_ids.reshape(entries)
    position = jnp.arange(entries, dtype=jnp.int32)
    earlier = (flat_ids[:, None] == flat_ids[None, :]) & (position[:, None] > position[None, :])
    ranks = jnp.sum(earlier, axis=1, dtype=jnp.int32)
    live = (jnp.arange(list_width, dtype=jnp.int32)[None, :] < live_counts[:, None]).reshape(entries)
    map_rows = -(-bucket // BLOCK)
    meta_at = -(-bucket // 16) * 16
    live_rows = tokens // BLOCK
    deep = meta_at + -(-(map_rows + live_rows) // 16) * 16
    rows = flat_ids // blocks * deep + ranks * blocks + flat_ids % blocks
    slots = jnp.arange(devices * deep, dtype=jnp.int32)
    place = (slots[:, None] == rows[None, :]).astype(jnp.bfloat16)
    send_teacher = jnp.dot(
        place, teacher.reshape(entries, BLOCK), preferred_element_type=jnp.float32
    ).astype(jnp.bfloat16)
    named = jnp.where(live, position // list_width + 1, 0)
    tight = flat_ids // blocks * bucket + ranks * blocks + flat_ids % blocks
    spots = jnp.arange(devices * bucket, dtype=jnp.int32)
    send_map = jnp.sum(jnp.where(tight[:, None] == spots[None, :], named[:, None], 0), axis=0)
    send_map = send_map.reshape(devices, bucket)
    send_map = jnp.pad(send_map, ((0, 0), (0, map_rows * BLOCK - bucket)))
    send_meta = jnp.concatenate(
        [
            send_map.reshape(devices, map_rows, BLOCK),
            jnp.broadcast_to(live_counts.reshape(1, live_rows, BLOCK), (devices, live_rows, BLOCK)),
            jnp.zeros((devices, deep - meta_at - map_rows - live_rows, BLOCK), jnp.int32),
        ],
        axis=1,
    ).astype(jnp.bfloat16)
    sent = lax.dynamic_update_slice(
        send_teacher.reshape(devices, deep, BLOCK), send_meta, (0, meta_at, 0)
    )
    lanes = jnp.stack([core, 1 - core])
    pair_of = chip_of.reshape(chips // 2, 1, 2)
    source_of = (pair_of // down * 2 + lanes[None, :, None]) * down + pair_of % down
    source_of = source_of.reshape(devices)
    if ring:
        sent = after(sent, *circle.moving, source_of)
        for number in range(2, chips // 2 - 1):
            circle.step(number)
    got = lax.all_to_all(sent, ALL, split_axis=0, concat_axis=0, tiled=True)

    got = got.at[source_of].get(mode="promise_in_bounds")
    meta = got[:, meta_at:].astype(jnp.int32)
    live_total = jnp.sum(meta[:, map_rows : map_rows + live_rows])
    scale = jnp.float32(tokens * devices) / live_total.astype(jnp.float32)
    slot_map = meta[:, :map_rows].reshape(devices, map_rows * BLOCK)[:, :bucket]
    slot_map = slot_map.reshape(quads, ROWS, blocks)
    offset = jnp.arange(ROWS, dtype=jnp.int32)[None, :, None] // C * tokens - 1
    slot_map = jnp.where(slot_map > 0, slot_map + offset, -1)
    slot_map = slot_map.swapaxes(1, 2).reshape(quads, blocks * ROWS)
    token_of = jnp.arange(QUAD * tokens, dtype=jnp.int32)
    pick = (slot_map[:, :, None] == token_of[None, None, :]).astype(jnp.bfloat16)
    if ring:
        circle.step(chips // 2 - 1, pick)
        held = [circle.got[int(offset)] for offset in offsets[:-1]]
    got_teacher = got[:, :bucket].reshape(devices, C, blocks, BLOCK)
    joint = 2 if turn % 2 == 0 else 1
    got_teacher = got_teacher.reshape(quads, ROWS, blocks // joint, joint, BLOCK)
    got_teacher = got_teacher.transpose(2, 0, 3, 1, 4).reshape(blocks * per_block, BLOCK)

    once = pl.Buffered(1)
    x_rows = blocks * ROWS
    part = max(n for n in range(1, 17) if blocks % n == 0 and (n * ROWS) % 16 == 0)
    placed = []
    runs = [[quad] for quad in range(quads)]
    if ring and quads > 2:
        runs = [list(range(quads - 2)), [quads - 2], [quads - 1]]
    for run in runs:
        if ring and run[-1] == quads - 1:
            circle.last(placed[: len(runs[0])], (*placed[len(runs[0]) :], got_teacher, scale))
            held += [circle.got[int(offset)] for offset in offsets[len(held) :]]
        operands = []
        for quad in run:
            two = held[quad * 2 : quad * 2 + 2]
            operands += [chip[lane] for lane in range(2) for chip in two]
        size = len(run)
        placed += call(
            place_kernel,
            f"place_{run[0]}",
            (blocks // part,),
            [
                pl.BlockSpec(
                    (size, part * ROWS, QUAD * tokens),
                    lambda s, q=run[0] // size: (q, s, 0),
                )
            ]
            + [pl.BlockSpec(o.shape, lambda s: (0, 0), pipeline_mode=once) for o in operands],
            [pl.BlockSpec((part * ROWS, width), lambda s: (s, 0))] * size,
            [jax.ShapeDtypeStruct((x_rows, width), jnp.bfloat16)] * size,
            2 * size * x_rows * QUAD * tokens * width,
            2 * size * x_rows * width * 2,
            52,
        )(pick, *operands)

    lane_slots = turn * per_block
    slot_spec = pl.BlockSpec((lane_slots, BLOCK), lambda s: (s, 0))
    flat_spec = pl.BlockSpec((BLOCK, lane_slots), lambda s: (0, s))
    x_spec = pl.BlockSpec((turn * ROWS, width), lambda s: (s, 0))
    flops = 2 * blocks * per_block * BLOCK * width
    if ring:
        part = (2 * tokens, width + LANES)
        out_specs = [pl.BlockSpec(part, lambda s: (0, 0), pipeline_mode=once)] * (2 * quads)
        out_shapes = [jax.ShapeDtypeStruct(part, jnp.bfloat16)] * (2 * quads)
        scratch = [
            pltpu.VMEM((blocks, per_block, width), jnp.float32),
            pltpu.VMEM((blocks, per_block, BLOCK), jnp.float32),
        ]
    else:
        out_specs = [
            pl.BlockSpec((turn, per_block, columns), lambda s: (s, 0, 0))
            for columns in (width, BLOCK)
        ]
        out_shapes = [
            jax.ShapeDtypeStruct((blocks, per_block, width), jnp.bfloat16),
            jax.ShapeDtypeStruct((blocks, per_block, BLOCK), jnp.float32),
        ]
        scratch = []
    grad, *results = call(
        functools.partial(main_kernel, turn, steps, quads, ring),
        "logits_and_back",
        (steps,),
        [
            pl.BlockSpec(memory_space=pltpu.SMEM),
            pl.BlockSpec((turn * BLOCK, width), lambda s: (s, 0)),
            slot_spec,
            pl.BlockSpec(slot_map.shape, lambda s: (0, 0), pipeline_mode=once),
        ]
        + [x_spec] * quads,
        [flat_spec] + out_specs,
        [jax.ShapeDtypeStruct((BLOCK, blocks * per_block), jnp.bfloat16)] + out_shapes,
        16 * flops,
        head.size * 2 + quads * x_rows * width * 2,
        52,
        scratch,
    )(
        scale.reshape(1),
        head,
        got_teacher,
        slot_map,
        *placed,
    )
    if ring:
        parts = results
    else:
        totals = []
        for value in results:
            value = value.astype(jnp.bfloat16).reshape(blocks, quads, ROWS, value.shape[-1])
            value = value.swapaxes(0, 1).reshape(quads, blocks * ROWS, value.shape[-1])
            totals.append(
                jnp.einsum("qst,qsd->qtd", pick, value, preferred_element_type=jnp.float32)
            )
        loss = totals[1]
        total = totals[0].astype(jnp.bfloat16).reshape(quads, 2, 2 * tokens, width)
        parts = [total[quad, lane] for lane in range(2) for quad in range(quads)]
    own_parts, other_parts = [], []
    for quad in range(quads):
        own_parts.append(parts[quad].reshape(2, tokens, -1))
        swapped = lax.ppermute(parts[quads + quad], "core", [(0, 1), (1, 0)])
        other_parts.append(swapped.reshape(2, tokens, -1))

    splits = 2 if turn % 4 == 0 else 1
    lots = min(steps * splits, chips - 1)
    cuts = [steps * splits * n // lots for n in range(lots + 1)]
    filled = []

    def fill(number, behind):
        shift = cuts[number]
        count = cuts[number + 1] - shift
        specs = [pl.BlockSpec((BLOCK, lane_slots), lambda s, d=shift: (0, (s + d) // splits))]
        specs += [
            pl.BlockSpec((turn * ROWS, width), lambda s, d=shift: ((s + d) // splits, 0))
        ] * quads
        operands = [grad if behind is None else after(grad, behind), *placed]
        aliases = {}
        if filled:
            specs.append(pl.BlockSpec(memory_space=pl.ANY))
            aliases = {len(operands): 0}
            operands.append(filled[-1])
        out, mark = call(
            functools.partial(head_kernel, turn, splits, shift, quads),
            f"head_grad_{number}",
            (count,),
            specs,
            [
                pl.BlockSpec((turn // splits * BLOCK, width), lambda s, d=shift: (s + d, 0)),
                pl.BlockSpec((8, LANES), lambda s: (0, 0)),
            ],
            [
                jax.ShapeDtypeStruct(head.shape, jnp.bfloat16),
                jax.ShapeDtypeStruct((8, LANES), jnp.float32),
            ],
            turn * flops // lots,
            (head.size + quads * x_rows * width) * 2 // lots,
            28,
            aliases=aliases,
        )(*operands)
        filled.append(out)
        return mark

    if ring:
        index_of = {int(o) % chips: n for n, o in enumerate(offsets)}
        half = width // 2
        sums, mark = [], None
        for step in range(1, chips + 1):
            operands, specs = [], []
            ends = [index_of[-step % chips], index_of[step % chips]]
            places = [(ends[0], half, 0), (ends[1], half, 1), (ends[0], LANES, width // LANES)]
            for source in (own_parts, other_parts):
                for at, columns, where in places:
                    operands.append(source[at // 2])
                    specs.append(
                        pl.BlockSpec(
                            (1, tokens, columns), lambda s, a=at % 2, w=where: (a, 0, w)
                        )
                    )
            for way in range(len(sums)):
                moved = lax.ppermute(sums[way], CHIPS, circle.ways[way])
                operands.append(moved if mark is None else after(moved, mark))
                specs.append(pl.BlockSpec(moved.shape, lambda s: (0, 0)))
            last = step == chips
            out_types = [(width, jnp.bfloat16), (LANES, jnp.float32)]
            if not last:
                out_types = [(half + LANES, jnp.bfloat16), (half, jnp.bfloat16)]
            sums = call(
                functools.partial(add_kernel, last),
                f"ring_sum_{step}",
                (1,),
                specs,
                [pl.BlockSpec((tokens, columns), lambda s: (0, 0)) for columns, _ in out_types],
                [jax.ShapeDtypeStruct((tokens, columns), kind) for columns, kind in out_types],
                len(operands) * tokens * half,
                len(operands) * tokens * half * 2,
                16,
            )(*operands)
            mark = fill(step - 1, sums[1]) if step <= lots else None
        hidden_grad, loss = sums
        token_loss = loss[:, 0]
    else:
        inverse = jnp.sum(
            jnp.where(source_of[None, :] == jnp.arange(devices)[:, None], jnp.arange(devices)[None], 0),
            axis=1,
        )
        loss = loss[:, :, 0].reshape(devices, tokens)
        loss = loss.at[inverse].get(mode="promise_in_bounds")
        loss = lax.all_to_all(loss, ALL, split_axis=0, concat_axis=0, tiled=True)
        token_loss = jnp.sum(loss, axis=0)
        total = [
            (own.astype(jnp.float32) + other.astype(jnp.float32)).astype(jnp.bfloat16)
            for own, other in zip(own_parts, other_parts)
        ]
        total = jnp.concatenate(total, axis=0).reshape(chips * tokens, width)
        hidden_grad = lax.psum_scatter(total, CHIPS, tiled=True)
        for number in range(lots):
            fill(number, None)
    head_grad = filled[-1]

    return hidden_grad, head_grad, token_loss


def solution(mesh):
    groups, tok, voc = (mesh.shape[name] for name in ("groups", "tok", "voc"))
    cores = Mesh(mesh.devices.reshape(groups, tok // 2, 2, voc), ("groups", "x", "core", "voc"))
    tokens_on = ("groups",) + ALL
    return jax.shard_map(
        on_device,
        mesh=cores,
        in_specs=(
            P(tokens_on, None),
            P(ALL, None),
            P(tokens_on, None),
            P(tokens_on),
            P(tokens_on, None, None),
        ),
        out_specs=(P(tokens_on, None), P(tokens_on, None), P(tokens_on)),
        check_vma=False,
    )
```

```python
import functools

import jax
import jax.numpy as jnp
import numpy as np
from jax import lax
from jax.experimental import pallas as pl
from jax.experimental.pallas import tpu as pltpu
from jax.sharding import Mesh
from jax.sharding import PartitionSpec as P

BLOCK = 128
LANES = 128
C = 2
QUAD = 4
ROWS = QUAD * C
COLS = 256
ALL = ("x", "core", "voc")
CHIPS = ("x", "voc")
RING_MOST = 8
MIB = 1024 * 1024
NT = (((1,), (1,)), ((), ()))


def call(kernel, name, grid, ins, outs, shapes, flops, moved, vmem, scratch=(), aliases=None):
    return pl.pallas_call(
        kernel,
        grid=grid,
        in_specs=ins,
        out_specs=outs,
        out_shape=shapes,
        scratch_shapes=scratch,
        input_output_aliases=aliases or {},
        compiler_params=pltpu.CompilerParams(
            dimension_semantics=("arbitrary",) * len(grid), vmem_limit_bytes=vmem * MIB
        ),
        cost_estimate=pl.CostEstimate(flops=flops, bytes_accessed=moved, transcendentals=0),
        name=name,
    )


def place_kernel(pick_ref, *refs):
    count = pick_ref.shape[0]
    held, outs = refs[: count * QUAD], refs[count * QUAD :]
    for start in range(0, outs[0].shape[1], COLS):
        columns = slice(start, start + COLS)
        for quad, out_ref in enumerate(outs):
            values = [ref[:, columns] for ref in held[quad * QUAD : (quad + 1) * QUAD]]
            rows = jnp.dot(
                pick_ref[quad], jnp.concatenate(values, axis=0), preferred_element_type=jnp.float32
            )
            out_ref[:, columns] = rows.astype(jnp.bfloat16)


def in_block(shape, axis, quads, joint):
    slot = lax.broadcasted_iota(jnp.int32, shape, axis)
    return slot // (quads * joint * ROWS) * joint + slot % (joint * ROWS) // ROWS


def joint_rows(x_refs, first, joint, columns=slice(None)):
    rows = slice(first * ROWS, (first + joint) * ROWS)
    return [ref[rows, columns] for ref in x_refs]


def sum_quad(spread, rows_ref, quad, columns):
    blocks = rows_ref.shape[0]
    rows = rows_ref[:, quad * ROWS : (quad + 1) * ROWS, columns]
    rows = rows.reshape(blocks * ROWS, rows.shape[-1]).astype(jnp.bfloat16)
    return jnp.dot(spread, rows, preferred_element_type=jnp.float32)


def two_parts(values):
    high = values.astype(jnp.bfloat16)
    low = (values - high.astype(jnp.float32)).astype(jnp.bfloat16)
    lane = lax.broadcasted_iota(jnp.int32, values.shape, 1)
    return jnp.where(lane < LANES // 2, high.astype(jnp.float32), low.astype(jnp.float32)).astype(
        jnp.bfloat16
    )


def joined(values):
    values = values.astype(jnp.float32)
    return values + pltpu.roll(values, LANES // 2, 1)


def main_kernel(turn, steps, quads, sums, scale_ref, head_ref, teacher_ref, map_ref, *refs):
    x_refs = refs[:quads]
    grad_ref, *loss_ref = refs[quads:-2]
    rows_ref, slot_loss_ref = refs[-2:]
    step = pl.program_id(0)
    origin = step * turn if sums else 0
    scale = scale_ref[0]
    joint = 2 if turn % 2 == 0 else 1
    group = quads * joint * ROWS
    own_block = in_block((group, BLOCK), 0, quads, joint)
    logits = []
    for first in range(0, turn, joint):
        product = lax.dot_general(
            jnp.concatenate(joint_rows(x_refs, first, joint), axis=0),
            head_ref[first * BLOCK : (first + joint) * BLOCK, :],
            NT,
            preferred_element_type=jnp.float32,
        )
        part = product[:, :BLOCK]
        for k in range(1, joint):
            part = jnp.where(own_block == k, product[:, k * BLOCK : (k + 1) * BLOCK], part)
        logits.append(part)
    logits = jnp.concatenate(logits, axis=0)

    def log_softmax(values):
        top = jnp.max(values, axis=-1, keepdims=True)
        return values - top - jnp.log(jnp.sum(jnp.exp(values - top), axis=-1, keepdims=True))

    student_log = log_softmax(logits)
    teacher_log = log_softmax(teacher_ref[...].astype(jnp.float32))
    teacher_prob = jnp.exp(teacher_log)
    loss = scale * jnp.sum(teacher_prob * (teacher_log - student_log), axis=-1, keepdims=True)
    loss = jnp.broadcast_to(loss, logits.shape)
    grad = BLOCK * scale * (jnp.exp(student_log) - teacher_prob)
    grad_ref[...] = grad.T.astype(jnp.bfloat16)
    grad = grad.astype(jnp.bfloat16)

    for first in range(0, turn, joint):
        here = slice(first * quads * ROWS, (first + joint) * quads * ROWS)
        lines = [
            jnp.where(own_block == k, grad[here], jnp.zeros_like(grad[here])) for k in range(joint)
        ]
        grads = jnp.dot(
            jnp.concatenate(lines, axis=1),
            head_ref[first * BLOCK : (first + joint) * BLOCK, :],
            preferred_element_type=jnp.float32,
        )
        for quad in range(quads):
            to = slice(quad * ROWS, (quad + 1) * ROWS)
            for k in range(joint):
                start = (quad * joint + k) * ROWS
                rows_ref[origin + first + k, to, :] = grads[start : start + ROWS].astype(
                    rows_ref.dtype
                )
                start += here.start
                slot_loss_ref[origin + first + k, to, :] = loss[start : start + ROWS]

    if not sums:
        return
    part_refs = loss_ref

    @pl.when(step == steps - 1)
    def _():
        half = part_refs[0].shape[0]
        width = rows_ref.shape[-1]
        for quad in range(quads):
            slots = map_ref[quad : quad + 1, :]
            token = lax.broadcasted_iota(jnp.int32, (2 * half, slots.shape[1]), 0)
            spread = jnp.where(slots == token, 1.0, 0.0).astype(jnp.bfloat16)

            def put(columns, total):
                part_refs[quad][:, columns] = total[:half]
                part_refs[quads + quad][:, columns] = total[half:]

            loss = sum_quad(spread, slot_loss_ref, quad, slice(0, LANES))
            put(slice(width, width + LANES), two_parts(loss))
            for start in range(0, width, COLS):
                columns = slice(start, start + COLS)
                put(columns, sum_quad(spread, rows_ref, quad, columns).astype(jnp.bfloat16))


def head_kernel(turn, splits, shift, quads, grad_ref, *refs):
    x_refs, (out_ref, mark_ref) = refs[:quads], refs[-2:]
    joint = 2 if turn % 2 == 0 else 1
    slots = grad_ref.shape[1]
    share = turn // splits
    place = in_block((1, slots), 1, quads, joint) - (pl.program_id(0) + shift) % splits * share
    grad = grad_ref[...]
    spaced = [grad * (place == index).astype(jnp.bfloat16) for index in range(share)]
    spaced = jnp.concatenate(spaced, axis=0)
    for start in range(0, out_ref.shape[1], COLS):
        columns = slice(start, start + COLS)
        rows = [
            piece
            for first in range(0, turn, joint)
            for piece in joint_rows(x_refs, first, joint, columns)
        ]
        out_ref[:, columns] = jnp.dot(
            spaced, jnp.concatenate(rows, axis=0), preferred_element_type=jnp.float32
        ).astype(jnp.bfloat16)
    mark_ref[...] = jnp.zeros_like(mark_ref)


def add_kernel(last, *refs):
    own_right, own_left, own_loss, other_right, other_left, other_loss = refs[:6]
    half = own_right.shape[-1]
    moved, outs = (refs[6:], ()) if len(refs) == 8 else (refs[6:8], refs[8:])
    moved, outs = (moved, outs) if outs else ((), moved)

    def whole(ref):
        return ref[...].reshape(ref.shape[-2:]).astype(jnp.float32)

    right = whole(own_right) + whole(other_right)
    left = whole(own_left) + whole(other_left)
    loss = joined(whole(own_loss)) + joined(whole(other_loss))
    if moved:
        right += moved[0][:, :half].astype(jnp.float32)
        left += moved[1][...].astype(jnp.float32)
        loss += joined(moved[0][:, half:])
    if last:
        outs[0][:, :half] = right.astype(jnp.bfloat16)
        outs[0][:, half:] = left.astype(jnp.bfloat16)
        outs[1][...] = loss
    else:
        outs[0][:, :half] = right.astype(jnp.bfloat16)
        outs[0][:, half:] = two_parts(loss)
        outs[1][...] = left.astype(jnp.bfloat16)


def ring_order(rows, columns):
    order = []
    for r in range(rows):
        line = [r * columns + c for c in range(columns)]
        order += line if r % 2 == 0 else line[::-1]
    return order


def arrivals(chips):
    near = [-1, 1, 0]
    for step in range(2, chips // 2):
        near += [-step, step]
    return near + [chips // 2]


def after(value, *others):
    return lax.optimization_barrier((value, *others))[0]


class Ring:
    def __init__(self, hidden, order):
        chips = len(order)
        self.order = order
        self.ways = [
            [(order[p], order[(p + way) % chips]) for p in range(chips)] for way in (1, -1)
        ]
        self.moving = [hidden, hidden]
        self.got = {0: self.both(hidden)}

    def both(self, shard):
        return shard, lax.ppermute(shard, "core", [(0, 1), (1, 0)])

    def step(self, number, *behind):
        if behind:
            self.moving = [after(shard, *behind) for shard in self.moving]
        self.moving = [lax.ppermute(shard, CHIPS, way) for shard, way in zip(self.moving, self.ways)]
        self.got[-number], self.got[number] = (self.both(shard) for shard in self.moving)

    def last(self, before, beside):
        shard = jnp.where(lax.axis_index("core") == 0, *self.moving)
        down = lax.axis_size("voc")

        def place(chip, core):
            return (chip // down * 2 + core) * down + chip % down

        links = [
            (place(source, core), place(target, core))
            for core in range(2)
            for source, target in self.ways[core]
        ]
        shard = lax.ppermute(after(shard, *before), ALL, links)
        self.got[len(self.order) // 2] = self.both(after(shard, *beside))


def gather_whole(hidden):
    chips = lax.axis_size(CHIPS)
    own = lax.all_gather(hidden, CHIPS, axis=0)
    other = lax.ppermute(own, "core", [(0, 1), (1, 0)])
    return [(own[chip], other[chip]) for chip in range(chips)]


def on_device(hidden, head, block_ids, live_counts, teacher):
    across, down = lax.axis_size("x"), lax.axis_size("voc")
    chips = across * down
    devices = 2 * chips
    quads = devices // QUAD
    tokens, list_width = block_ids.shape
    width = hidden.shape[1]
    blocks = head.shape[0] // BLOCK
    even = [n for n in range(2, 9, 2) if blocks % n == 0]
    turn = max(even) if even else 1
    steps = blocks // turn
    entries = tokens * list_width
    bucket = blocks * C
    per_block = devices * C
    core = lax.axis_index("core")
    ring = chips <= RING_MOST
    order = ring_order(across, down)
    if ring:
        circle = Ring(hidden, order)
        circle.step(1)
        offsets = np.array(arrivals(chips))

        def turned(place):
            line, spot = place // down, place % down
            return line * down + jnp.where(line % 2 == 0, spot, down - 1 - spot)

        chip_of = turned((turned(lax.axis_index(CHIPS)) + offsets + chips) % chips)
    else:
        held = gather_whole(hidden)
        offsets = np.arange(chips)
        chip_of = jnp.arange(chips, dtype=jnp.int32)

    flat_ids = block_ids.reshape(entries)
    position = jnp.arange(entries, dtype=jnp.int32)
    earlier = (flat_ids[:, None] == flat_ids[None, :]) & (position[:, None] > position[None, :])
    ranks = jnp.sum(earlier, axis=1, dtype=jnp.int32)
    live = (jnp.arange(list_width, dtype=jnp.int32)[None, :] < live_counts[:, None]).reshape(entries)
    map_rows = -(-bucket // BLOCK)
    meta_at = -(-bucket // 16) * 16
    live_rows = tokens // BLOCK
    deep = meta_at + -(-(map_rows + live_rows) // 16) * 16
    rows = flat_ids // blocks * deep + ranks * blocks + flat_ids % blocks
    slots = jnp.arange(devices * deep, dtype=jnp.int32)
    place = (slots[:, None] == rows[None, :]).astype(jnp.bfloat16)
    send_teacher = jnp.dot(
        place, teacher.reshape(entries, BLOCK), preferred_element_type=jnp.float32
    ).astype(jnp.bfloat16)
    named = jnp.where(live, position // list_width + 1, 0)
    tight = flat_ids // blocks * bucket + ranks * blocks + flat_ids % blocks
    spots = jnp.arange(devices * bucket, dtype=jnp.int32)
    send_map = jnp.sum(jnp.where(tight[:, None] == spots[None, :], named[:, None], 0), axis=0)
    send_map = send_map.reshape(devices, bucket)
    send_map = jnp.pad(send_map, ((0, 0), (0, map_rows * BLOCK - bucket)))
    send_meta = jnp.concatenate(
        [
            send_map.reshape(devices, map_rows, BLOCK),
            jnp.broadcast_to(live_counts.reshape(1, live_rows, BLOCK), (devices, live_rows, BLOCK)),
            jnp.zeros((devices, deep - meta_at - map_rows - live_rows, BLOCK), jnp.int32),
        ],
        axis=1,
    ).astype(jnp.bfloat16)
    sent = lax.dynamic_update_slice(
        send_teacher.reshape(devices, deep, BLOCK), send_meta, (0, meta_at, 0)
    )
    lanes = jnp.stack([core, 1 - core])
    pair_of = chip_of.reshape(chips // 2, 1, 2)
    source_of = (pair_of // down * 2 + lanes[None, :, None]) * down + pair_of % down
    source_of = source_of.reshape(devices)
    if ring:
        sent = after(sent, *circle.moving, source_of)
        for number in range(2, chips // 2 - 1):
            circle.step(number)
    got = lax.all_to_all(sent, ALL, split_axis=0, concat_axis=0, tiled=True)

    got = got.at[source_of].get(mode="promise_in_bounds")
    meta = got[:, meta_at:].astype(jnp.int32)
    live_total = jnp.sum(meta[:, map_rows : map_rows + live_rows])
    scale = jnp.float32(tokens * devices) / live_total.astype(jnp.float32)
    slot_map = meta[:, :map_rows].reshape(devices, map_rows * BLOCK)[:, :bucket]
    slot_map = slot_map.reshape(quads, ROWS, blocks)
    offset = jnp.arange(ROWS, dtype=jnp.int32)[None, :, None] // C * tokens - 1
    slot_map = jnp.where(slot_map > 0, slot_map + offset, -1)
    slot_map = slot_map.swapaxes(1, 2).reshape(quads, blocks * ROWS)
    token_of = jnp.arange(QUAD * tokens, dtype=jnp.int32)
    pick = (slot_map[:, :, None] == token_of[None, None, :]).astype(jnp.bfloat16)
    if ring:
        circle.step(chips // 2 - 1, pick)
        held = [circle.got[int(offset)] for offset in offsets[:-1]]
    got_teacher = got[:, :bucket].reshape(devices, C, blocks, BLOCK)
    joint = 2 if turn % 2 == 0 else 1
    got_teacher = got_teacher.reshape(quads, ROWS, blocks // joint, joint, BLOCK)
    got_teacher = got_teacher.transpose(2, 0, 3, 1, 4).reshape(blocks * per_block, BLOCK)

    once = pl.Buffered(1)
    x_rows = blocks * ROWS
    part = max(n for n in range(1, 17) if blocks % n == 0 and (n * ROWS) % 16 == 0)
    placed = []
    runs = [[quad] for quad in range(quads)]
    if ring and quads > 2:
        runs = [list(range(quads - 2)), [quads - 2], [quads - 1]]
    for run in runs:
        if ring and run[-1] == quads - 1:
            first = len(runs[0])
            circle.last((*placed[:first], got_teacher, scale), placed[first:])
            held += [circle.got[int(offset)] for offset in offsets[len(held) :]]
        operands = []
        for quad in run:
            two = held[quad * 2 : quad * 2 + 2]
            operands += [chip[lane] for lane in range(2) for chip in two]
        size = len(run)
        placed += call(
            place_kernel,
            f"place_{run[0]}",
            (blocks // part,),
            [
                pl.BlockSpec(
                    (size, part * ROWS, QUAD * tokens),
                    lambda s, q=run[0] // size: (q, s, 0),
                )
            ]
            + [pl.BlockSpec(o.shape, lambda s: (0, 0), pipeline_mode=once) for o in operands],
            [pl.BlockSpec((part * ROWS, width), lambda s: (s, 0))] * size,
            [jax.ShapeDtypeStruct((x_rows, width), jnp.bfloat16)] * size,
            2 * size * x_rows * QUAD * tokens * width,
            2 * size * x_rows * width * 2,
            52,
        )(pick, *operands)

    lane_slots = turn * per_block
    slot_spec = pl.BlockSpec((lane_slots, BLOCK), lambda s: (s, 0))
    flat_spec = pl.BlockSpec((BLOCK, lane_slots), lambda s: (0, s))
    x_spec = pl.BlockSpec((turn * ROWS, width), lambda s: (s, 0))
    flops = 2 * blocks * per_block * BLOCK * width
    if ring:
        part = (2 * tokens, width + LANES)
        out_specs = [pl.BlockSpec(part, lambda s: (0, 0), pipeline_mode=once)] * (2 * quads)
        out_shapes = [jax.ShapeDtypeStruct(part, jnp.bfloat16)] * (2 * quads)
        scratch = [
            pltpu.VMEM((blocks, per_block, width), jnp.float32),
            pltpu.VMEM((blocks, per_block, BLOCK), jnp.float32),
        ]
    else:
        out_specs = [
            pl.BlockSpec((turn, per_block, columns), lambda s: (s, 0, 0))
            for columns in (width, BLOCK)
        ]
        out_shapes = [
            jax.ShapeDtypeStruct((blocks, per_block, width), jnp.bfloat16),
            jax.ShapeDtypeStruct((blocks, per_block, BLOCK), jnp.float32),
        ]
        scratch = []
    grad, *results = call(
        functools.partial(main_kernel, turn, steps, quads, ring),
        "logits_and_back",
        (steps,),
        [
            pl.BlockSpec(memory_space=pltpu.SMEM),
            pl.BlockSpec((turn * BLOCK, width), lambda s: (s, 0)),
            slot_spec,
            pl.BlockSpec(slot_map.shape, lambda s: (0, 0), pipeline_mode=once),
        ]
        + [x_spec] * quads,
        [flat_spec] + out_specs,
        [jax.ShapeDtypeStruct((BLOCK, blocks * per_block), jnp.bfloat16)] + out_shapes,
        16 * flops,
        head.size * 2 + quads * x_rows * width * 2,
        52,
        scratch,
    )(
        scale.reshape(1),
        head,
        got_teacher,
        slot_map,
        *placed,
    )
    if ring:
        parts = results
    else:
        totals = []
        for value in results:
            value = value.astype(jnp.bfloat16).reshape(blocks, quads, ROWS, value.shape[-1])
            value = value.swapaxes(0, 1).reshape(quads, blocks * ROWS, value.shape[-1])
            totals.append(
                jnp.einsum("qst,qsd->qtd", pick, value, preferred_element_type=jnp.float32)
            )
        loss = totals[1]
        total = totals[0].astype(jnp.bfloat16).reshape(quads, 2, 2 * tokens, width)
        parts = [total[quad, lane] for lane in range(2) for quad in range(quads)]
    own_parts, other_parts = [], []
    for quad in range(quads):
        own_parts.append(parts[quad].reshape(2, tokens, -1))
        swapped = lax.ppermute(parts[quads + quad], "core", [(0, 1), (1, 0)])
        other_parts.append(swapped.reshape(2, tokens, -1))

    splits = 2 if turn % 4 == 0 else 1
    lots = min(steps * splits, chips - 1)
    cuts = [steps * splits * n // lots for n in range(lots + 1)]
    filled = []

    def fill(number, behind):
        shift = cuts[number]
        count = cuts[number + 1] - shift
        specs = [pl.BlockSpec((BLOCK, lane_slots), lambda s, d=shift: (0, (s + d) // splits))]
        specs += [
            pl.BlockSpec((turn * ROWS, width), lambda s, d=shift: ((s + d) // splits, 0))
        ] * quads
        operands = [grad if behind is None else after(grad, behind), *placed]
        aliases = {}
        if filled:
            specs.append(pl.BlockSpec(memory_space=pl.ANY))
            aliases = {len(operands): 0}
            operands.append(filled[-1])
        out, mark = call(
            functools.partial(head_kernel, turn, splits, shift, quads),
            f"head_grad_{number}",
            (count,),
            specs,
            [
                pl.BlockSpec((turn // splits * BLOCK, width), lambda s, d=shift: (s + d, 0)),
                pl.BlockSpec((8, LANES), lambda s: (0, 0)),
            ],
            [
                jax.ShapeDtypeStruct(head.shape, jnp.bfloat16),
                jax.ShapeDtypeStruct((8, LANES), jnp.float32),
            ],
            turn * flops // lots,
            (head.size + quads * x_rows * width) * 2 // lots,
            28,
            aliases=aliases,
        )(*operands)
        filled.append(out)
        return mark

    if ring:
        index_of = {int(o) % chips: n for n, o in enumerate(offsets)}
        half = width // 2
        sums, mark = [], None
        for step in range(1, chips + 1):
            operands, specs = [], []
            ends = [index_of[-step % chips], index_of[step % chips]]
            places = [(ends[0], half, 0), (ends[1], half, 1), (ends[0], LANES, width // LANES)]
            for source in (own_parts, other_parts):
                for at, columns, where in places:
                    operands.append(source[at // 2])
                    specs.append(
                        pl.BlockSpec(
                            (1, tokens, columns), lambda s, a=at % 2, w=where: (a, 0, w)
                        )
                    )
            for way in range(len(sums)):
                moved = lax.ppermute(sums[way], CHIPS, circle.ways[way])
                operands.append(moved if mark is None else after(moved, mark))
                specs.append(pl.BlockSpec(moved.shape, lambda s: (0, 0)))
            last = step == chips
            out_types = [(width, jnp.bfloat16), (LANES, jnp.float32)]
            if not last:
                out_types = [(half + LANES, jnp.bfloat16), (half, jnp.bfloat16)]
            sums = call(
                functools.partial(add_kernel, last),
                f"ring_sum_{step}",
                (1,),
                specs,
                [pl.BlockSpec((tokens, columns), lambda s: (0, 0)) for columns, _ in out_types],
                [jax.ShapeDtypeStruct((tokens, columns), kind) for columns, kind in out_types],
                len(operands) * tokens * half,
                len(operands) * tokens * half * 2,
                16,
            )(*operands)
            mark = fill(step - 1, sums[1]) if step <= lots else None
        hidden_grad, loss = sums
        token_loss = loss[:, 0]
    else:
        inverse = jnp.sum(
            jnp.where(source_of[None, :] == jnp.arange(devices)[:, None], jnp.arange(devices)[None], 0),
            axis=1,
        )
        loss = loss[:, :, 0].reshape(devices, tokens)
        loss = loss.at[inverse].get(mode="promise_in_bounds")
        loss = lax.all_to_all(loss, ALL, split_axis=0, concat_axis=0, tiled=True)
        token_loss = jnp.sum(loss, axis=0)
        total = [
            (own.astype(jnp.float32) + other.astype(jnp.float32)).astype(jnp.bfloat16)
            for own, other in zip(own_parts, other_parts)
        ]
        total = jnp.concatenate(total, axis=0).reshape(chips * tokens, width)
        hidden_grad = lax.psum_scatter(total, CHIPS, tiled=True)
        for number in range(lots):
            fill(number, None)
    head_grad = filled[-1]

    return hidden_grad, head_grad, token_loss


def solution(mesh):
    groups, tok, voc = (mesh.shape[name] for name in ("groups", "tok", "voc"))
    cores = Mesh(mesh.devices.reshape(groups, tok // 2, 2, voc), ("groups", "x", "core", "voc"))
    tokens_on = ("groups",) + ALL
    return jax.shard_map(
        on_device,
        mesh=cores,
        in_specs=(
            P(tokens_on, None),
            P(ALL, None),
            P(tokens_on, None),
            P(tokens_on),
            P(tokens_on, None, None),
        ),
        out_specs=(P(tokens_on, None), P(tokens_on, None), P(tokens_on)),
        check_vma=False,
    )
```
